768 devices in a mesh: tile: 48 (over z_lo, y, core), layer: 16 (over z_hi, x).
Axes of the slice: x: 4, y: 8, z: 12 (z_hi: 4, z_lo: 3; z = z_hi * 3 + z_lo), core: 2. Of those that a mesh axis runs over, the one named last changes fastest.
Arguments:
- adjoint: float32 [32, 2, 384, 2048], P('layer', None, 'tile'), may hold values from -6 to 6
- source: float32 [32, 2, 384, 2048], P('layer', None, 'tile'), may hold values from -6 to 6
- viscosity: float32 [32, 384, 2048], P('layer', 'tile'), may hold values from 0.3 to 3
- vertical: float32 [32, 384, 2048], P(None, 'tile', 'layer'), may hold values from 1 to 30
- friction: float32 [384, 2048], P('tile', 'layer'), may hold values from 0.1 to 10
- ice_mask: int32 [384, 2048], P('tile', 'layer'), may hold values 0 or 1
- gate_cells: int32 [1536, 64], P('layer'), may hold values from 0 to 786431
- gate_owner: int32 [1536], replicated, may hold values from 0 to 767, as said below
Outputs:
- adjoint_new: float32 [32, 2, 384, 2048], P('layer', None, 'tile')
- gate_flux: float32 [768, 2], P(('tile', 'layer'))
The draws below stay inside these ranges and needn't reach their ends.
Inputs may be any that keep to these rules, and one draw needn't show every extreme that they name: `gate_owner`: every owner id appears exactly 2 times.
All inputs are finite; a program needn't handle non-finite values. No bound on the sum of `ice_mask` on one device may be relied on, other than what follows from the above.
Results may differ from the reference program's by a relative error of at most 0.000028.
Values sent between devices are 32-bit elements; how exact they have to be, the bound alone decides.
A program may use at most 32 MiB of HBM per device.

```python
import math
import jax
import jax.numpy as jnp
from jax import lax

GCELLS = 64
SLOTS = 2
NX = 384
NY = 2048
NZ = 32
OWNERS = 768
GATES = 1536


def draw_gate_owner(key, part):
    order_index = jax.random.permutation(key, GATES)
    return (order_index % OWNERS).astype(jnp.int32)


def with_ends(values, stream_key, low, largest):
    longest = values.shape.index(max(values.shape))
    spots = []
    for shift in (0, 1):
        where = [jax.random.randint(jax.random.fold_in(stream_key, axis), (), 0, length) for axis, length in enumerate(values.shape)]
        where[longest] = (where[longest] + shift) % values.shape[longest]
        spots.append(tuple(where))
    return values.at[spots[0]].set(low).at[spots[1]].set(largest)


def block_scale(stream_key, dims, split, low, high):
    def one(axis_at, shards_of):
        heights = jax.random.uniform(jax.random.fold_in(jax.random.fold_in(stream_key, 6), axis_at), (shards_of,), jnp.float32, low / len(split), high / len(split))
        return jnp.repeat(jnp.exp(heights), dims[axis_at] // shards_of).reshape((-1,) + (1,) * (len(dims) - axis_at - 1))

    gain = one(*split[0])
    for cut in split[1:]:
        gain = gain * one(*cut)
    return gain


def centred(own_key, dims, spread, most, shards=(), dtype=jnp.bfloat16):
    entries = spread * jax.random.normal(own_key, dims, jnp.float32)
    if shards:
        entries = entries * block_scale(own_key, dims, shards, -0.22, 0.18)
    return jnp.clip(entries, -most, most).astype(dtype)


def setup_inputs(seed: int = 0) -> dict:
    streams_of = jax.random.split(jax.random.key(seed), 9)
    return {
        "adjoint": centred(streams_of[0], (NZ, 2, NX, NY), 1.0, 6.0, ((0, 16), (2, 48)), jnp.float32),
        "source": centred(streams_of[1], (NZ, 2, NX, NY), 1.0, 6.0, ((0, 16), (2, 48)), jnp.float32),
        "viscosity": jnp.clip(jnp.exp(math.log(3.0) - 2.3025851 * jax.random.uniform(streams_of[2], (NZ, NX, NY), jnp.float32) ** block_scale(streams_of[2], (NZ, NX, NY), ((0, 16), (1, 48)), -0.2, 0.2)), 0.3, 3.0),
        "vertical": jnp.clip(jnp.exp(math.log(30.0) - 3.4011974 * jax.random.uniform(streams_of[3], (NZ, NX, NY), jnp.float32) ** block_scale(streams_of[3], (NZ, NX, NY), ((1, 48), (2, 16)), -0.2, 0.2)), 1.0, 30.0),
        "friction": jnp.clip(jnp.exp(math.log(10.0) - 4.6051702 * jax.random.uniform(streams_of[4], (NX, NY), jnp.float32) ** block_scale(streams_of[4], (NX, NY), ((0, 48), (1, 16)), -0.2, 0.2)), 0.1, 10.0),
        "ice_mask": with_ends((jax.random.randint(streams_of[5], (NX, NY), 0, 4) < 3).astype(jnp.int32), jax.random.fold_in(streams_of[5], 1), 0, 1),
        "gate_cells": with_ends(jax.random.randint(streams_of[6], (GATES, GCELLS), 0, NX * NY), jax.random.fold_in(streams_of[6], 1), 0, (NX * NY) - 1).astype(jnp.int32),
        "gate_owner": draw_gate_owner(jax.random.fold_in(streams_of[8], 71), 0),
    }


step_scale = 0.2


def stencil(padded, viscosity):
    centre = padded[:, :, 1:-1, 1:-1]
    beside = padded[:, :, 2:, 1:-1] + padded[:, :, :-2, 1:-1] + padded[:, :, 1:-1, 2:] + padded[:, :, 1:-1, :-2]
    cross_term = 0.25 * (padded[:, :, 2:, 2:] - padded[:, :, 2:, :-2] - padded[:, :, :-2, 2:] + padded[:, :, :-2, :-2])
    return viscosity[:, None] * (beside - 4.0 * centre + cross_term[:, ::-1])


def column_solve(rhs, vertical, friction):
    zero_plane = jnp.zeros_like(friction)

    def forward(state, layer_terms):
        below_prev, link_prev, ratio_prev, scaled_prev = state
        vert_k, rhs_k = layer_terms
        diag_k = 1.0 + below_prev + vert_k
        pivot_value = diag_k - link_prev * ratio_prev
        ratio_new = vert_k / pivot_value
        scaled_new = (rhs_k + link_prev[None] * scaled_prev) / pivot_value[None]
        return (vert_k, vert_k, ratio_new, scaled_new), (ratio_new, scaled_new)

    initial = (friction, zero_plane, zero_plane, jnp.zeros_like(rhs[0]))
    _, (ratios, scaled) = lax.scan(forward, initial, (vertical, rhs))

    def backward(upper_value, layer_terms):
        ratio_k, scaled_k = layer_terms
        solved_value = scaled_k + ratio_k[None] * upper_value
        return solved_value, solved_value

    _, solved = lax.scan(backward, jnp.zeros_like(rhs[0]), (ratios, scaled), reverse=True)
    return solved


def owner_order(gate_owner):
    return jnp.argsort(gate_owner, stable=True).astype(jnp.int32)


def reference(adjoint, source, viscosity, vertical, friction, ice_mask, gate_cells, gate_owner):
    padded = jnp.pad(adjoint, ((0, 0), (0, 0), (1, 1), (1, 1)))
    rhs = source + step_scale * stencil(padded, viscosity)
    solved = column_solve(rhs, vertical, friction) * ice_mask.astype(jnp.float32)[None, None]
    discharge = jnp.sum(solved, axis=(0, 1)) / NZ
    gate_total = jnp.sum(discharge.reshape(-1)[gate_cells], axis=1)
    owner_table = gate_total[owner_order(gate_owner)]
    return solved, owner_table.reshape(OWNERS, SLOTS)
```

```python
import functools

import jax
import jax.numpy as jnp
from jax import lax
from jax.experimental import pallas as pl
from jax.experimental.pallas import tpu as pltpu
from jax.sharding import PartitionSpec as P

MESH = pl.DeviceIdType.MESH
SCALE = 0.2
F32 = jnp.float32


def remote(src, dst, send_sem, recv_sem, axis, peer):
    return pltpu.make_async_remote_copy(
        src_ref=src,
        dst_ref=dst,
        send_sem=send_sem,
        recv_sem=recv_sem,
        device_id={axis: peer},
        device_id_type=MESH,
    )


def kernel(
    tiles,
    layers,
    adjoint_in,
    source_in,
    viscosity_in,
    vertical_in,
    friction_in,
    mask_in,
    cells_in,
    owner_in,
    out,
    flux,
    adjoint,
    source,
    viscosity,
    vertical,
    friction,
    mask,
    cells,
    owner,
    halo,
    rhs,
    gathered,
    solved,
    inverse,
    ratio,
    table,
    select,
    block_cells,
    cell_rows_out,
    cell_rows_in,
    gate_rows,
    picked,
    parts,
    load_sem,
    halo_send,
    halo_recv,
    rhs_send,
    rhs_recv,
    back_send,
    back_recv,
    table_send,
    table_recv,
    own_send,
    own_recv,
    rows_send,
    rows_recv,
    part_send,
    part_recv,
    self_sem,
):
    tile = lax.axis_index("tile")
    layer = lax.axis_index("layer")
    nz = vertical.shape[0]
    per_layer = nz // layers
    width = rhs.shape[3]
    rows = rhs.shape[2]

    def ring(axis, me, size, step):
        return lax.rem(me + step, size)

    barrier = pltpu.get_barrier_semaphore()

    def greet(axis, me, size):
        def one(step, carry):
            pl.semaphore_signal(
                barrier, inc=1, device_id={axis: lax.rem(me + step, size)}, device_id_type=MESH
            )
            return carry

        lax.fori_loop(1, size, one, 0)

    greet("layer", layer, layers)
    greet("tile", tile, tiles)

    loads = []
    for i, (a, b) in enumerate(
        (
            (adjoint_in, adjoint),
            (source_in, source),
            (viscosity_in, viscosity),
            (vertical_in, vertical),
            (friction_in, friction),
            (mask_in, mask),
            (cells_in, cells),
            (owner_in, owner),
        )
    ):
        copy = pltpu.make_async_copy(a, b, load_sem.at[i])
        copy.start()
        loads.append(copy)

    loads[0].wait()
    pl.semaphore_wait(barrier, layers - 1 + tiles - 1)

    up, down = lax.rem(tile + tiles - 1, tiles), lax.rem(tile + 1, tiles)
    to_down = remote(
        adjoint.at[:, :, pl.ds(rows - 1, 1)], halo.at[0], halo_send.at[0], halo_recv.at[0], "tile", down
    )
    to_up = remote(
        adjoint.at[:, :, pl.ds(0, 1)], halo.at[1], halo_send.at[1], halo_recv.at[1], "tile", up
    )
    to_down.start()
    to_up.start()

    for c in loads[1:]:
        c.wait()
    lane = lax.broadcasted_iota(jnp.int32, (1, width), 1)
    first_col, last_col = lane == 0, lane == width - 1
    sub = lax.broadcasted_iota(jnp.int32, (rows, 1), 0)

    def sideways(a):
        left = jnp.where(first_col, 0.0, pltpu.roll(a, 1, 1))
        right = jnp.where(last_col, 0.0, pltpu.roll(a, width - 1, 1))
        return left, right

    for k in range(per_layer):
        coef = SCALE * viscosity[k]
        value, diff, flat = [], [], []
        for c in range(2):
            a = adjoint[k, c]
            left, right = sideways(a)
            value.append(a)
            diff.append(0.25 * (right - left))
            flat.append(left + right - 4.0 * a)
        for c in range(2):
            above = jnp.where(sub == 0, 0.0, pltpu.roll(value[c] - diff[1 - c], 1, 0))
            below = jnp.where(sub == rows - 1, 0.0, pltpu.roll(value[c] + diff[1 - c], rows - 1, 0))
            rhs[k, c] = source[k, c] + coef * (flat[c] + (above + below))

    count = cells.shape[0]
    gates = owner.shape[0] * 128
    owner_ids = tile * layers + lax.broadcasted_iota(jnp.int32, (layers, 128), 0)
    lane128 = lax.broadcasted_iota(jnp.int32, (layers, 128), 1)
    far = jnp.full((layers, 128), gates, jnp.int32)
    for j in range(owner.shape[0]):
        mine = owner[pl.ds(j, 1), :] == owner_ids
        far = jnp.minimum(far, jnp.where(mine, lane128 + j * 128, gates))
    first = jnp.min(far, axis=1, keepdims=True)
    for j in range(owner.shape[0]):
        mine = owner[pl.ds(j, 1), :] == owner_ids
        is_first = (lane128 + j * 128) == first
        select[0:layers, j * 128 : (j + 1) * 128] = jnp.where(mine & is_first, 1.0, 0.0)
        select[layers : 2 * layers, j * 128 : (j + 1) * 128] = jnp.where(
            mine & jnp.logical_not(is_first), 1.0, 0.0
        )
    select[:, gates:] = jnp.zeros((2 * layers, select.shape[1] - gates), F32)
    base = (layer * count) // 128
    shift = layer * count - base * 128
    block_cells[...] = jnp.zeros_like(block_cells)
    block_cells[pl.ds(pl.multiple_of(shift, 32), count), :] = cells[...].astype(F32)
    chosen = jnp.dot(
        select[:, pl.ds(pl.multiple_of(base * 128, 128), 256)],
        block_cells[...],
        precision=lax.Precision.HIGHEST,
        preferred_element_type=F32,
    )
    cell_rows_out[...] = jnp.concatenate([chosen[0:layers], chosen[layers:]], axis=1)

    def own_copy(step):
        peer = lax.rem(layer + step, layers)
        return remote(
            cell_rows_out.at[pl.ds(peer, 1)],
            cell_rows_in.at[pl.ds(layer, 1)],
            own_send.at[step - 1],
            own_recv.at[step - 1],
            "layer",
            peer,
        )

    def each(size, fn):
        def one(step, carry):
            fn(step)
            return carry

        lax.fori_loop(1, size, one, 0)

    to_down.wait_recv()
    to_up.wait_recv()
    has_up, has_down = tile > 0, tile < tiles - 1
    lane_w = lax.broadcasted_iota(jnp.int32, (1, width), 1)
    for k in range(per_layer):
        top_coef = SCALE * viscosity[k, 0:1]
        low_coef = SCALE * viscosity[k, rows - 1 : rows]
        for c in range(2):
            o = 1 - c
            left, right = sideways(halo[0, k, o])
            above = halo[0, k, c] - 0.25 * (right - left)
            rhs[k, c, 0:1] += jnp.where(has_up, top_coef * above, 0.0)
            left, right = sideways(halo[1, k, o])
            below = halo[1, k, c] + 0.25 * (right - left)
            rhs[k, c, rows - 1 : rows] += jnp.where(has_down, low_coef * below, 0.0)

    def rhs_copy(step):
        peer = lax.rem(layer + step, layers)
        return remote(
            rhs.at[:, :, :, pl.ds(pl.multiple_of(peer * 128, 128), 128)],
            gathered.at[pl.ds(layer * per_layer, per_layer)],
            rhs_send.at[step - 1],
            rhs_recv.at[step - 1],
            "layer",
            peer,
        )

    each(layers, lambda s: rhs_copy(s).start())
    each(layers, lambda s: own_copy(s).start())
    for k in range(per_layer):
        for c in range(2):
            gathered[layer * per_layer + k, c] = rhs[
                k, c, :, pl.ds(pl.multiple_of(layer * 128, 128), 128)
            ]
    cell_rows_in[pl.ds(layer, 1)] = cell_rows_out[pl.ds(layer, 1)]

    active = mask[...].astype(F32)
    beneath = friction[...]
    link = jnp.zeros_like(beneath)
    ratio_prev = jnp.zeros_like(beneath)
    for k in range(nz):
        v = vertical[k]
        inv = 1.0 / (1.0 + beneath + v - link * ratio_prev)
        ratio_prev = v * inv
        inverse[k] = inv
        ratio[k] = ratio_prev
        beneath = v
        link = v

    each(layers, lambda s: own_copy(s).wait_recv())
    gate_rows[pl.ds(tile, 1)] = jnp.sum(cell_rows_in[...], axis=0, keepdims=True)

    def rows_copy(step):
        return remote(
            gate_rows.at[pl.ds(tile, 1)],
            gate_rows.at[pl.ds(tile, 1)],
            rows_send.at[step - 1],
            rows_recv.at[step - 1],
            "tile",
            lax.rem(tile + step, tiles),
        )

    each(tiles, lambda s: rows_copy(s).start())

    each(layers, lambda s: rhs_copy(s).wait_recv())
    scaled = [jnp.zeros((rows, 128), F32)] * 2
    for k in range(nz):
        inv = inverse[k]
        for c in range(2):
            if k:
                scaled[c] = (gathered[k, c] + vertical[k - 1] * scaled[c]) * inv
            else:
                scaled[c] = gathered[k, c] * inv
            solved[k, c] = scaled[c]
    upper = [jnp.zeros((rows, 128), F32)] * 2
    total = jnp.zeros((rows, 128), F32)
    for k in reversed(range(nz)):
        for c in range(2):
            upper[c] = solved[k, c] + ratio[k] * upper[c] if k < nz - 1 else solved[k, c]
            x = upper[c] * active
            solved[k, c] = x
            total = total + x
    table[layer] = total * (1.0 / nz)

    def table_copy(step):
        return remote(
            table.at[layer],
            table.at[layer],
            table_send.at[step - 1],
            table_recv.at[step - 1],
            "layer",
            lax.rem(layer + step, layers),
        )

    each(layers, lambda s: table_copy(s).start())

    def back_copy(step):
        peer = lax.rem(layer + step, layers)
        return remote(
            solved.at[pl.ds(peer * per_layer, per_layer)],
            out.at[:, :, :, pl.ds(pl.multiple_of(layer * 128, 128), 128)],
            back_send.at[step - 1],
            back_recv.at[step - 1],
            "layer",
            peer,
        )

    each(layers, lambda s: back_copy(s).start())
    keep = pltpu.make_async_copy(
        solved.at[pl.ds(layer * per_layer, per_layer)],
        out.at[:, :, :, pl.ds(pl.multiple_of(layer * 128, 128), 128)],
        self_sem,
    )
    keep.start()

    each(tiles, lambda s: rows_copy(s).wait_recv())
    where, lanes = [], []
    groups = tiles // 8
    for v in range(groups):
        cell = gate_rows[v * 8 : (v + 1) * 8].astype(jnp.int32)
        row, col = cell // width, cell % width
        here = (row // rows) == tile
        where.append(jnp.where(here, (col // 128) * rows + row % rows, -1))
        lanes.append(col % 128)

    each(layers, lambda s: table_copy(s).wait_recv())
    found = [jnp.zeros((8, 128), F32)] * groups
    for l in range(layers):
        for r in range(rows):
            line = jnp.broadcast_to(table[l, r : r + 1], (8, 128))
            for v in range(groups):
                got = jnp.take_along_axis(line, lanes[v], axis=1, mode="promise_in_bounds")
                found[v] = jnp.where(where[v] == l * rows + r, got, found[v])
    for v in range(groups):
        picked[v * 8 : (v + 1) * 8] = found[v]

    def part_copy(step):
        peer = lax.rem(tile + step, tiles)
        return remote(
            picked.at[pl.ds(peer, 1)],
            parts.at[pl.ds(tile, 1)],
            part_send.at[step - 1],
            part_recv.at[step - 1],
            "tile",
            peer,
        )

    each(tiles, lambda s: part_copy(s).start())
    parts[pl.ds(tile, 1)] = picked[pl.ds(tile, 1)]
    each(tiles, lambda s: part_copy(s).wait_recv())
    line = jnp.sum(parts[...], axis=0, keepdims=True)
    half = lax.broadcasted_iota(jnp.int32, (1, 128), 1) < 64
    low = jnp.sum(jnp.where(half, line, 0.0), axis=1, keepdims=True)
    high = jnp.sum(jnp.where(half, 0.0, line), axis=1, keepdims=True)
    flux[...] = jnp.where(lax.broadcasted_iota(jnp.int32, (1, 2), 1) == 0, low, high)

    each(layers, lambda s: back_copy(s).wait_recv())
    keep.wait()
    to_down.wait_send()
    to_up.wait_send()

    def sent(step):
        own_copy(step).wait_send()
        rhs_copy(step).wait_send()
        table_copy(step).wait_send()
        back_copy(step).wait_send()

    each(layers, sent)

    def sent_tile(step):
        rows_copy(step).wait_send()
        part_copy(step).wait_send()

    each(tiles, sent_tile)


def solution(mesh):
    tiles, layers = mesh.shape["tile"], mesh.shape["layer"]

    def local(adjoint, source, viscosity, vertical, friction, ice_mask, gate_cells, gate_owner):
        owner = gate_owner.reshape(-1, 128)
        per_layer, _, rows, width = adjoint.shape
        nz = vertical.shape[0]
        vmem, dma = pltpu.VMEM, pltpu.SemaphoreType.DMA
        scratch = [
            vmem(a.shape, a.dtype)
            for a in (adjoint, source, viscosity, vertical, friction, ice_mask, gate_cells, owner)
        ]
        scratch += [
            vmem((2, per_layer, 2, 1, width), F32),
            vmem(adjoint.shape, F32),
            vmem((nz, 2, rows, 128), F32),
            vmem((nz, 2, rows, 128), F32),
            vmem((nz, rows, 128), F32),
            vmem((nz, rows, 128), F32),
            vmem((layers, rows, 128), F32),
            vmem((2 * layers, owner.size + 128), F32),
            vmem((256, gate_cells.shape[1]), F32),
            vmem((layers, 128), F32),
            vmem((layers, 128), F32),
            vmem((tiles, 128), F32),
            vmem((tiles, 128), F32),
            vmem((tiles, 128), F32),
            dma((8,)),
        ]
        for n in (2, layers - 1, layers - 1, layers - 1, layers - 1, tiles - 1, tiles - 1):
            scratch += [dma((n,)), dma((n,))]
        scratch += [dma]
        return pl.pallas_call(
            functools.partial(kernel, tiles, layers),
            out_shape=(
                jax.ShapeDtypeStruct(adjoint.shape, F32),
                jax.ShapeDtypeStruct((1, 2), F32),
            ),
            in_specs=[pl.BlockSpec(memory_space=pl.ANY)] * 8,
            out_specs=(
                pl.BlockSpec(memory_space=pl.ANY),
                pl.BlockSpec(memory_space=pltpu.VMEM),
            ),
            scratch_shapes=scratch,
            compiler_params=pltpu.CompilerParams(
                collective_id=0, has_side_effects=True, vmem_limit_bytes=32 * 1024 * 1024
            ),
            name="update",
        )(adjoint, source, viscosity, vertical, friction, ice_mask, gate_cells, owner)

    return jax.shard_map(
        local,
        mesh=mesh,
        in_specs=(
            P("layer", None, "tile", None),
            P("layer", None, "tile", None),
            P("layer", "tile", None),
            P(None, "tile", "layer"),
            P("tile", "layer"),
            P("tile", "layer"),
            P("layer", None),
            P(),
        ),
        out_specs=(P("layer", None, "tile", None), P(("tile", "layer"), None)),
        check_vma=False,
    )
```

```python
import functools

import jax
import jax.numpy as jnp
from jax import lax
from jax.experimental import pallas as pl
from jax.experimental.pallas import tpu as pltpu
from jax.sharding import PartitionSpec as P

MESH = pl.DeviceIdType.MESH
SCALE = 0.2
F32 = jnp.float32


NX, NY, ZLO, ZHI, NC = 4, 8, 3, 4, 2


def remote(src, dst, send_sem, recv_sem, device):
    return pltpu.make_async_remote_copy(
        src_ref=src,
        dst_ref=dst,
        send_sem=send_sem,
        recv_sem=recv_sem,
        device_id=device,
        device_id_type=MESH,
    )


def kernel(
    tiles,
    layers,
    adjoint_in,
    source_in,
    viscosity_in,
    vertical_in,
    friction_in,
    mask_in,
    cells_in,
    owner_in,
    out,
    flux,
    adjoint,
    source,
    viscosity,
    vertical,
    friction,
    mask,
    cells,
    owner,
    halo,
    rhs,
    edge,
    gathered,
    edges_in,
    solved,
    inverse,
    ratio,
    table,
    select,
    block_cells,
    cell_rows_out,
    cell_rows_in,
    gate_rows,
    picked,
    parts,
    load_sem,
    halo_send,
    halo_recv,
    rhs_send,
    rhs_recv,
    edge_send,
    edge_recv,
    back_send,
    back_recv,
    own_send,
    own_recv,
    table_send,
    table_recv,
    rows_send,
    rows_recv,
    part_send,
    part_recv,
    self_sem,
    halo_ready,
    layer_ready,
    late_ready,
):
    tile = lax.axis_index("tile")
    layer = lax.axis_index("layer")
    nz = vertical.shape[0]
    per_layer = nz // layers
    width = rhs.shape[3]
    rows = rhs.shape[2]
    core, y, z_lo = tile % NC, (tile // NC) % NY, tile // (NC * NY)
    x, z_hi = layer % NX, layer // NX
    xy = y * NX + x
    zc = (z_hi * ZLO + z_lo) * NC + core
    n_xy, n_zc = NX * NY, ZHI * ZLO * NC
    y_rank = jnp.where(y < NY // 2, y, NY + NY // 2 - 1 - y)

    def loop(low, high, fn):
        def one(i, carry):
            fn(i)
            return carry

        lax.fori_loop(low, high, one, 0)

    def at_xy(q):
        qy, qx = q // NX, q % NX
        return {"tile": (z_lo * NY + qy) * NC + core, "layer": z_hi * NX + qx}

    def at_zc(q):
        qc, qz = q % NC, q // NC
        return {"tile": ((qz % ZLO) * NY + y) * NC + qc, "layer": (qz // ZLO) * NX + x}

    def at_layer(p):
        return {"tile": tile, "layer": p}

    def other_y(q):
        return q // NX != y

    def other_zc(q):
        return jnp.logical_or(q % NC != core, (q // NC) % ZLO != z_lo)

    def signal(sem, device):
        pl.semaphore_signal(sem, inc=1, device_id=device, device_id_type=MESH)

    loads = []
    for i, (a, b) in enumerate(
        (
            (adjoint_in, adjoint),
            (source_in, source),
            (viscosity_in, viscosity),
            (vertical_in, vertical),
            (friction_in, friction),
            (mask_in, mask),
            (cells_in, cells),
            (owner_in, owner),
        )
    ):
        copy = pltpu.make_async_copy(a, b, load_sem.at[i])
        copy.start()
        loads.append(copy)

    barrier = pltpu.get_barrier_semaphore()
    has_up, has_down = tile > 0, tile < tiles - 1

    @pl.when(has_down)
    def _():
        signal(barrier, {"tile": tile + 1, "layer": layer})

    loop(layer + 1, layers, lambda p: signal(barrier, at_layer(p)))

    def greet_xy(q):
        qy = q // NX
        rank = jnp.where(qy < NY // 2, qy, NY + NY // 2 - 1 - qy)

        @pl.when(rank > y_rank)
        def _():
            signal(barrier, at_xy(q))

    loop(0, n_xy, greet_xy)

    def greet_zc(q):
        @pl.when(other_zc(q))
        def _():
            signal(barrier, at_zc(q))

    loop(zc + 1, n_zc, greet_zc)

    for c in loads:
        c.wait()
    lane = lax.broadcasted_iota(jnp.int32, (1, width), 1)
    first_col, last_col = lane == 0, lane == width - 1
    sub = lax.broadcasted_iota(jnp.int32, (rows, 1), 0)

    def sideways(a):
        left = jnp.where(first_col, 0.0, pltpu.roll(a, 1, 1))
        right = jnp.where(last_col, 0.0, pltpu.roll(a, width - 1, 1))
        return left, right

    for k in range(per_layer):
        coef = SCALE * viscosity[k]
        value, diff, flat = [], [], []
        for c in range(2):
            a = adjoint[k, c]
            left, right = sideways(a)
            value.append(a)
            diff.append(0.25 * (right - left))
            flat.append(left + right - 4.0 * a)
        for c in range(2):
            above = jnp.where(sub == 0, 0.0, pltpu.roll(value[c] - diff[1 - c], 1, 0))
            below = jnp.where(sub == rows - 1, 0.0, pltpu.roll(value[c] + diff[1 - c], rows - 1, 0))
            r = source[k, c] + coef * (flat[c] + (above + below))
            rhs[k, c] = r
            edge[k, c, 0:1] = r[0:1]
            edge[k, c, 1:2] = r[rows - 1 : rows]

    count = cells.shape[1]
    gates = owner.shape[0] * 128
    owner_ids = tile * layers + lax.broadcasted_iota(jnp.int32, (layers, 128), 0)
    lane128 = lax.broadcasted_iota(jnp.int32, (layers, 128), 1)
    far = jnp.full((layers, 128), gates, jnp.int32)
    for j in range(owner.shape[0]):
        mine = owner[pl.ds(j, 1), :] == owner_ids
        far = jnp.minimum(far, jnp.where(mine, lane128 + j * 128, gates))
    first = jnp.min(far, axis=1, keepdims=True)
    for j in range(owner.shape[0]):
        mine = owner[pl.ds(j, 1), :] == owner_ids
        is_first = (lane128 + j * 128) == first
        select[0:layers, j * 128 : (j + 1) * 128] = jnp.where(mine & is_first, 1.0, 0.0)
        select[layers : 2 * layers, j * 128 : (j + 1) * 128] = jnp.where(
            mine & jnp.logical_not(is_first), 1.0, 0.0
        )
    select[:, gates:] = jnp.zeros((2 * layers, select.shape[1] - gates), F32)
    base = (layer * count) // 128
    shift = layer * count - base * 128
    block_cells[...] = jnp.zeros_like(block_cells)
    block_cells[:, 0:count] = cells[...].astype(F32)
    window = select[:, pl.ds(pl.multiple_of(base * 128, 128), 256)]
    window = pltpu.roll(window, lax.rem(256 - shift, 256), 1)[:, 0:128]
    chosen = lax.dot_general(
        window,
        block_cells[...],
        (((1,), (1,)), ((), ())),
        precision=lax.Precision.HIGHEST,
        preferred_element_type=F32,
    )
    cell_rows_out[...] = jnp.concatenate([chosen[0:layers], chosen[layers:]], axis=1)
    cell_rows_in[pl.ds(layer, 1)] = cell_rows_out[pl.ds(layer, 1)]

    active = mask[...].astype(F32)
    beneath = friction[...]
    link = jnp.zeros_like(beneath)
    ratio_prev = jnp.zeros_like(beneath)
    for k in range(nz):
        v = vertical[k]
        inv = 1.0 / (1.0 + beneath + v - link * ratio_prev)
        ratio_prev = v * inv
        inverse[k] = inv
        ratio[k] = ratio_prev
        beneath = v
        link = v

    lower = layer + y_rank * NX + zc - z_hi + has_up.astype(jnp.int32)

    @pl.when(lower > 0)
    def _():
        pl.semaphore_wait(barrier, lower)

    @pl.when(has_up)
    def _():
        signal(halo_ready, {"tile": tile - 1, "layer": layer})

    loop(0, layer, lambda p: signal(layer_ready.at[layer], at_layer(p)))

    to_down = remote(
        adjoint.at[:, :, pl.ds(rows - 1, 1)],
        halo.at[0],
        halo_send.at[0],
        halo_recv.at[0],
        {"tile": tile + 1, "layer": layer},
    )
    to_up = remote(
        adjoint.at[:, :, pl.ds(0, 1)],
        halo.at[1],
        halo_send.at[1],
        halo_recv.at[1],
        {"tile": tile - 1, "layer": layer},
    )

    @pl.when(has_up)
    def _():
        to_up.start()

    def answer_xy(q):
        qy = q // NX
        rank = jnp.where(qy < NY // 2, qy, NY + NY // 2 - 1 - qy)

        @pl.when(rank < y_rank)
        def _():
            signal(late_ready, at_xy(q))

    def answer_zc(q):
        @pl.when(other_zc(q))
        def _():
            signal(late_ready, at_zc(q))

    def rhs_copy(peer, slot):
        return remote(
            rhs.at[:, :, pl.ds(1, rows - 2), pl.ds(pl.multiple_of(peer * 128, 128), 128)],
            gathered.at[pl.ds(layer * per_layer, per_layer), :, pl.ds(1, rows - 2)],
            rhs_send.at[peer],
            rhs_recv.at[slot],
            at_layer(peer),
        )

    def own_copy(peer, slot):
        return remote(
            cell_rows_out.at[pl.ds(peer, 1)],
            cell_rows_in.at[pl.ds(layer, 1)],
            own_send.at[peer],
            own_recv.at[slot],
            at_layer(peer),
        )

    def edge_copy(peer, slot):
        return remote(
            edge.at[:, :, :, pl.ds(pl.multiple_of(peer * 128, 128), 128)],
            edges_in.at[pl.ds(layer * per_layer, per_layer)],
            edge_send.at[peer],
            edge_recv.at[slot],
            at_layer(peer),
        )

    def send_rhs(s):
        peer = jnp.where(s <= layer, layer - s, s)

        @pl.when(s > layer)
        def _():
            pl.semaphore_wait(layer_ready.at[peer], 1)

        rhs_copy(peer, layer).start()
        own_copy(peer, layer).start()

    loop(1, layer + 1, send_rhs)
    loop(0, n_xy, answer_xy)
    loop(0, zc, answer_zc)

    @pl.when(has_down)
    def _():
        pl.semaphore_wait(halo_ready, 1)
        to_down.start()

    loop(layer + 1, layers, send_rhs)

    def beside(side, row, sign):
        for k in range(per_layer):
            factor = SCALE * viscosity[k, row : row + 1]
            for c in range(2):
                left, right = sideways(halo[side, k, 1 - c])
                term = halo[side, k, c] + (sign * 0.25) * (right - left)
                edge[k, c, side : side + 1] += factor * term

    @pl.when(has_up)
    def _():
        to_down.wait_recv()
        beside(0, 0, -1.0)

    @pl.when(has_down)
    def _():
        to_up.wait_recv()
        beside(1, rows - 1, 1.0)

    def other_layers(fn):
        def one(s):
            fn(lax.rem(layer + s, layers))

        loop(1, layers, one)

    other_layers(lambda p: edge_copy(p, layer).start())
    here = pl.ds(pl.multiple_of(layer * 128, 128), 128)
    for k in range(per_layer):
        for c in range(2):
            gathered[layer * per_layer + k, c] = rhs[k, c, :, here]
            edges_in[layer * per_layer + k, c] = edge[k, c, :, here]

    other_layers(lambda p: own_copy(p, p).wait_recv())
    gate_rows[pl.ds(zc, 1)] = jnp.sum(cell_rows_in[...], axis=0, keepdims=True)
    answers = (NY - 1 - y_rank) * NX + (n_zc - 1 - zc) - (ZHI - 1 - z_hi)

    @pl.when(answers > 0)
    def _():
        pl.semaphore_wait(late_ready, answers)

    def others(size, me, fn):
        def one(s):
            fn(lax.rem(me + s, size))

        loop(1, size, one)

    def rows_copy(q, slot):
        return remote(
            gate_rows.at[pl.ds(zc, 1)], gate_rows.at[pl.ds(zc, 1)], rows_send.at[q], rows_recv.at[slot], at_zc(q)
        )

    others(n_zc, zc, lambda q: rows_copy(q, zc).start())

    other_layers(lambda p: rhs_copy(p, p).wait_recv())
    other_layers(lambda p: edge_copy(p, p).wait_recv())
    row_of = lax.broadcasted_iota(jnp.int32, (rows, 128), 0)
    top, low = row_of == 0, row_of == rows - 1
    scaled = [jnp.zeros((rows, 128), F32)] * 2
    for k in range(nz):
        inv = inverse[k]
        for c in range(2):
            r = jnp.where(low, edges_in[k, c, 1:2], gathered[k, c])
            r = jnp.where(top, edges_in[k, c, 0:1], r)
            scaled[c] = (r + vertical[k - 1] * scaled[c]) * inv if k else r * inv
            solved[k, c] = scaled[c]
    upper = [jnp.zeros((rows, 128), F32)] * 2
    total = jnp.zeros((rows, 128), F32)
    for k in reversed(range(nz)):
        for c in range(2):
            upper[c] = solved[k, c] + ratio[k] * upper[c] if k < nz - 1 else solved[k, c]
            x_new = upper[c] * active
            solved[k, c] = x_new
            total = total + x_new
    table[xy] = total * (1.0 / nz)

    def table_copy(q, slot):
        return remote(table.at[xy], table.at[xy], table_send.at[q], table_recv.at[slot], at_xy(q))

    others(n_xy, xy, lambda q: table_copy(q, xy).start())

    def back_copy(peer, slot):
        return remote(
            solved.at[pl.ds(peer * per_layer, per_layer)],
            out.at[:, :, :, here],
            back_send.at[peer],
            back_recv.at[slot],
            at_layer(peer),
        )

    other_layers(lambda p: back_copy(p, layer).start())
    keep = pltpu.make_async_copy(solved.at[pl.ds(layer * per_layer, per_layer)], out.at[:, :, :, here], self_sem)
    keep.start()

    others(n_zc, zc, lambda q: rows_copy(q, q).wait_recv())
    groups = n_zc // 8
    where, lanes = [], []
    for v in range(groups):
        cell = gate_rows[v * 8 : (v + 1) * 8].astype(jnp.int32)
        row, col = cell // width, cell % width
        t, piece = row // rows, col // 128
        inside = (t % NC == core) & (t // (NC * NY) == z_lo) & (piece // NX == z_hi)
        spot = (((t // NC) % NY) * NX + piece % NX) * rows + row % rows
        where.append(jnp.where(inside, spot, -1))
        lanes.append(col % 128)

    def look(s, found):
        q = lax.rem(xy + s, n_xy)

        @pl.when(s > 0)
        def _():
            table_copy(q, q).wait_recv()

        found = list(found)
        for r in range(rows):
            line = jnp.broadcast_to(table[q, r : r + 1], (8, 128))
            for v in range(groups):
                got = jnp.take_along_axis(line, lanes[v], axis=1, mode="promise_in_bounds")
                found[v] = jnp.where(where[v] == q * rows + r, got, found[v])
        return tuple(found)

    found = lax.fori_loop(0, n_xy, look, tuple(jnp.zeros((8, 128), F32) for _ in range(groups)))
    for v in range(groups):
        picked[v * 8 : (v + 1) * 8] = found[v]

    def part_copy(q, slot):
        return remote(
            picked.at[pl.ds(q, 1)], parts.at[pl.ds(zc, 1)], part_send.at[q], part_recv.at[slot], at_zc(q)
        )

    others(n_zc, zc, lambda q: part_copy(q, zc).start())
    parts[pl.ds(zc, 1)] = picked[pl.ds(zc, 1)]
    others(n_zc, zc, lambda q: part_copy(q, q).wait_recv())
    line = jnp.sum(parts[...], axis=0, keepdims=True)
    half = lax.broadcasted_iota(jnp.int32, (1, 128), 1) < 64
    slot0 = jnp.sum(jnp.where(half, line, 0.0), axis=1, keepdims=True)
    slot1 = jnp.sum(jnp.where(half, 0.0, line), axis=1, keepdims=True)
    flux[...] = jnp.where(lax.broadcasted_iota(jnp.int32, (1, 2), 1) == 0, slot0, slot1)

    other_layers(lambda p: back_copy(p, p).wait_recv())
    keep.wait()

    @pl.when(has_up)
    def _():
        to_up.wait_send()

    @pl.when(has_down)
    def _():
        to_down.wait_send()

    def sent(p):
        rhs_copy(p, p).wait_send()
        edge_copy(p, p).wait_send()
        own_copy(p, p).wait_send()
        back_copy(p, p).wait_send()

    other_layers(sent)
    others(n_xy, xy, lambda q: table_copy(q, q).wait_send())

    def sent_zc(q):
        rows_copy(q, q).wait_send()
        part_copy(q, q).wait_send()

    others(n_zc, zc, sent_zc)


def solution(mesh):
    tiles, layers = mesh.shape["tile"], mesh.shape["layer"]
    n_xy, n_zc = NX * NY, ZHI * ZLO * NC
    assert tiles == ZLO * NY * NC and layers == ZHI * NX

    def local(adjoint, source, viscosity, vertical, friction, ice_mask, gate_cells, gate_owner):
        owner = gate_owner.reshape(-1, 128)
        gate_cells = gate_cells.T
        per_layer, _, rows, width = adjoint.shape
        nz = vertical.shape[0]
        vmem, dma = pltpu.VMEM, pltpu.SemaphoreType.DMA
        scratch = [
            vmem(a.shape, a.dtype)
            for a in (adjoint, source, viscosity, vertical, friction, ice_mask, gate_cells, owner)
        ]
        scratch += [
            vmem((2, per_layer, 2, 1, width), F32),
            vmem(adjoint.shape, F32),
            vmem((per_layer, 2, 2, width), F32),
            vmem((nz, 2, rows, 128), F32),
            vmem((nz, 2, 2, 128), F32),
            vmem((nz, 2, rows, 128), F32),
            vmem((nz, rows, 128), F32),
            vmem((nz, rows, 128), F32),
            vmem((n_xy, rows, 128), F32),
            vmem((2 * layers, owner.size + 128), F32),
            vmem((gate_cells.shape[0], 128), F32),
            vmem((layers, 128), F32),
            vmem((layers, 128), F32),
            vmem((n_zc, 128), F32),
            vmem((n_zc, 128), F32),
            vmem((n_zc, 128), F32),
            dma((8,)),
        ]
        for n in (2, layers, layers, layers, layers, n_xy, n_zc, n_zc):
            scratch += [dma((n,)), dma((n,))]
        plain = pltpu.SemaphoreType.REGULAR
        scratch += [dma, plain, plain((layers,)), plain]
        return pl.pallas_call(
            functools.partial(kernel, tiles, layers),
            out_shape=(
                jax.ShapeDtypeStruct(adjoint.shape, F32),
                jax.ShapeDtypeStruct((1, 2), F32),
            ),
            in_specs=[pl.BlockSpec(memory_space=pltpu.HBM)] * 8,
            out_specs=(
                pl.BlockSpec(memory_space=pl.ANY),
                pl.BlockSpec(memory_space=pltpu.VMEM),
            ),
            scratch_shapes=scratch,
            compiler_params=pltpu.CompilerParams(
                collective_id=0, has_side_effects=True, vmem_limit_bytes=60 * 1024 * 1024
            ),
            name="update",
        )(adjoint, source, viscosity, vertical, friction, ice_mask, gate_cells, owner)

    return jax.shard_map(
        local,
        mesh=mesh,
        in_specs=(
            P("layer", None, "tile", None),
            P("layer", None, "tile", None),
            P("layer", "tile", None),
            P(None, "tile", "layer"),
            P("tile", "layer"),
            P("tile", "layer"),
            P("layer", None),
            P(),
        ),
        out_specs=(P("layer", None, "tile", None), P(("tile", "layer"), None)),
        check_vma=False,
    )
```

```python
import functools

import jax
import jax.numpy as jnp
from jax import lax
from jax.experimental import pallas as pl
from jax.experimental.pallas import tpu as pltpu
from jax.sharding import PartitionSpec as P

MESH = pl.DeviceIdType.MESH
SCALE = 0.2
F32 = jnp.float32


NX, NY, ZLO, ZHI, NC = 4, 8, 3, 4, 2


def remote(src, dst, send_sem, recv_sem, device):
    return pltpu.make_async_remote_copy(
        src_ref=src,
        dst_ref=dst,
        send_sem=send_sem,
        recv_sem=recv_sem,
        device_id=device,
        device_id_type=MESH,
    )


def kernel(
    tiles,
    layers,
    adjoint_in,
    source_in,
    viscosity_in,
    vertical_in,
    friction_in,
    mask_in,
    cells_in,
    owner_in,
    out,
    flux,
    adjoint,
    source,
    viscosity,
    vertical,
    friction,
    mask,
    cells,
    owner,
    halo,
    rims,
    rhs,
    gathered,
    solved,
    inverse,
    ratio,
    table,
    select,
    block_cells,
    cell_rows_out,
    cell_rows_in,
    gate_rows,
    picked,
    parts,
    load_sem,
    halo_send,
    halo_recv,
    rhs_send,
    rhs_recv,
    back_send,
    back_recv,
    own_send,
    own_recv,
    table_send,
    table_recv,
    rows_send,
    rows_recv,
    part_send,
    part_recv,
    self_sem,
    halo_ready,
    layer_ready,
    late_ready,
):
    tile = lax.axis_index("tile")
    layer = lax.axis_index("layer")
    nz = vertical.shape[0]
    per_layer = nz // layers
    width = rhs.shape[3]
    rows = rhs.shape[2]
    core, y, z_lo = tile % NC, (tile // NC) % NY, tile // (NC * NY)
    x, z_hi = layer % NX, layer // NX
    xy = y * NX + x
    zc = (z_hi * ZLO + z_lo) * NC + core
    n_xy, n_zc = NX * NY, ZHI * ZLO * NC

    def loop(low, high, fn):
        def one(i, carry):
            fn(i)
            return carry

        lax.fori_loop(low, high, one, 0)

    def at_layer(s):
        return {"tile": tile, "layer": layer ^ s}

    def at_xy(s):
        return {"tile": tile ^ ((s >> 2) << 1), "layer": layer ^ (s & (NX - 1))}

    def zc_parts(j):
        z = z_lo + (j >> 3)
        return z_hi ^ (j & 3), jnp.where(z >= ZLO, z - ZLO, z), core ^ ((j >> 2) & 1)

    def zc_index(j):
        high, low, c = zc_parts(j)
        return (high * ZLO + low) * NC + c

    def at_zc(j):
        _, low, c = zc_parts(j)
        return {"tile": low * (NY * NC) + (tile & (NY * NC - NC)) + c, "layer": layer ^ ((j & 3) << 2)}

    def rank_of(a):
        return jnp.where(a < NY // 2, a, NY + NY // 2 - 1 - a)

    def signal(sem, device):
        pl.semaphore_signal(sem, inc=1, device_id=device, device_id_type=MESH)

    def arrived(ref, sem):
        pltpu.make_async_copy(ref, ref, sem).wait()

    y_rank = rank_of(y)
    loads = []
    for i, (a, b) in enumerate(
        (
            (adjoint_in, adjoint),
            (source_in, source),
            (viscosity_in, viscosity),
            (vertical_in, vertical),
            (friction_in, friction),
            (mask_in, mask),
            (cells_in, cells),
            (owner_in, owner),
        )
    ):
        copy = pltpu.make_async_copy(a, b, load_sem.at[i])
        copy.start()
        loads.append(copy)

    barrier = pltpu.get_barrier_semaphore()
    has_up, has_down = tile > 0, tile < tiles - 1

    @pl.when(has_down)
    def _():
        signal(barrier, {"tile": tile + 1, "layer": layer})

    def greet_layer(s):
        @pl.when(layer ^ s > layer)
        def _():
            signal(barrier, at_layer(s))

    loop(1, layers, greet_layer)

    def greet_xy(s):
        @pl.when(rank_of(y ^ (s >> 2)) > y_rank)
        def _():
            signal(barrier, at_xy(s))

    loop(NX, n_xy, greet_xy)

    def greet_zc(j):
        @pl.when(zc_index(j) > zc)
        def _():
            signal(barrier, at_zc(j))

    loop(ZHI, n_zc, greet_zc)

    lower = layer + y_rank * NX + zc - z_hi + has_up.astype(jnp.int32)

    @pl.when(lower > 0)
    def _():
        pl.semaphore_wait(barrier, lower)

    @pl.when(has_up)
    def _():
        signal(halo_ready, {"tile": tile - 1, "layer": layer})

    def answer_layer(s):
        @pl.when(layer ^ s < layer)
        def _():
            signal(layer_ready.at[s], at_layer(s))

    loop(layers // 2, layers, answer_layer)
    loop(1, layers // 2, answer_layer)

    to_down = remote(
        rims.at[1],
        halo.at[0],
        halo_send.at[0],
        halo_recv.at[0],
        {"tile": tile + 1, "layer": layer},
    )
    to_up = remote(
        rims.at[0],
        halo.at[1],
        halo_send.at[1],
        halo_recv.at[1],
        {"tile": tile - 1, "layer": layer},
    )
    loads[0].wait()
    for side, row in enumerate((0, rows - 1)):
        for k in range(per_layer):
            for c in range(2):
                rims[side, 2 * k + c : 2 * k + c + 1] = adjoint[k, c, row : row + 1]

    @pl.when(has_up)
    def _():
        to_up.start()

    loads[1].wait()
    loads[2].wait()
    lane = lax.broadcasted_iota(jnp.int32, (1, width), 1)
    first_col, last_col = lane == 0, lane == width - 1
    sub = lax.broadcasted_iota(jnp.int32, (rows, 1), 0)

    def sideways(a):
        left = jnp.where(first_col, 0.0, pltpu.roll(a, 1, 1))
        right = jnp.where(last_col, 0.0, pltpu.roll(a, width - 1, 1))
        return left, right

    for k in range(per_layer):
        coef = SCALE * viscosity[k]
        value, diff, flat = [], [], []
        for c in range(2):
            a = adjoint[k, c]
            left, right = sideways(a)
            value.append(a)
            diff.append(0.25 * (right - left))
            flat.append(left + right - 4.0 * a)
        for c in range(2):
            above = jnp.where(sub == 0, 0.0, pltpu.roll(value[c] - diff[1 - c], 1, 0))
            below = jnp.where(sub == rows - 1, 0.0, pltpu.roll(value[c] + diff[1 - c], rows - 1, 0))
            rhs[k, c] = source[k, c] + coef * (flat[c] + (above + below))

    def rhs_copy(s):
        peer = layer ^ s
        return remote(
            rhs.at[:, :, :, pl.ds(pl.multiple_of(peer * 128, 128), 128)],
            gathered.at[pl.ds(layer * per_layer, per_layer)],
            rhs_send,
            rhs_recv,
            at_layer(s),
        )

    def own_copy(s):
        return remote(
            cell_rows_out.at[pl.ds(layer ^ s, 1)],
            cell_rows_in.at[pl.ds(layer, 1)],
            own_send,
            own_recv,
            at_layer(s),
        )

    def send_low(s):
        @pl.when(layer ^ s < layer)
        def _():
            rhs_copy(s).start()


    def answer_xy(s):
        @pl.when(rank_of(y ^ (s >> 2)) < y_rank)
        def _():
            signal(late_ready, at_xy(s))

    def answer_zc(j):
        @pl.when(zc_index(j) < zc)
        def _():
            signal(late_ready, at_zc(j))

    loop(NX, n_xy, answer_xy)
    loop(ZHI, n_zc, answer_zc)

    for c in loads[3:]:
        c.wait()
    count = cells.shape[1]
    gates = owner.shape[0] * 128
    owner_ids = tile * layers + lax.broadcasted_iota(jnp.int32, (layers, 128), 0)
    lane128 = lax.broadcasted_iota(jnp.int32, (layers, 128), 1)
    far = jnp.full((layers, 128), gates, jnp.int32)
    for j in range(owner.shape[0]):
        mine = owner[pl.ds(j, 1), :] == owner_ids
        far = jnp.minimum(far, jnp.where(mine, lane128 + j * 128, gates))
    first = jnp.min(far, axis=1, keepdims=True)
    for j in range(owner.shape[0]):
        mine = owner[pl.ds(j, 1), :] == owner_ids
        is_first = (lane128 + j * 128) == first
        select[0:layers, j * 128 : (j + 1) * 128] = jnp.where(mine & is_first, 1.0, 0.0)
        select[layers : 2 * layers, j * 128 : (j + 1) * 128] = jnp.where(
            mine & jnp.logical_not(is_first), 1.0, 0.0
        )
    select[:, gates:] = jnp.zeros((2 * layers, select.shape[1] - gates), F32)
    base = (layer * count) // 128
    shift = layer * count - base * 128
    block_cells[...] = jnp.zeros_like(block_cells)
    block_cells[:, 0:count] = cells[...].astype(F32)
    window = select[:, pl.ds(pl.multiple_of(base * 128, 128), 256)]
    window = pltpu.roll(window, lax.rem(256 - shift, 256), 1)[:, 0:128]
    chosen = lax.dot_general(
        window,
        block_cells[...],
        (((1,), (1,)), ((), ())),
        precision=lax.Precision.HIGHEST,
        preferred_element_type=F32,
    )
    cell_rows_out[...] = jnp.concatenate([chosen[0:layers], chosen[layers:]], axis=1)
    cell_rows_in[pl.ds(layer, 1)] = cell_rows_out[pl.ds(layer, 1)]

    active = mask[...].astype(F32)
    beneath = friction[...]
    link = jnp.zeros_like(beneath)
    ratio_prev = jnp.zeros_like(beneath)
    for k in range(nz):
        v = vertical[k]
        inv = 1.0 / (1.0 + beneath + v - link * ratio_prev)
        ratio_prev = v * inv
        inverse[k] = inv
        ratio[k] = ratio_prev
        beneath = v
        link = v

    @pl.when(has_down)
    def _():
        pl.semaphore_wait(halo_ready, 1)
        to_down.start()

    def beside(side, row, sign):
        for k in range(per_layer):
            factor = SCALE * viscosity[k, row : row + 1]
            for c in range(2):
                left, right = sideways(halo[side, 2 * k + 1 - c : 2 * k + 2 - c])
                term = halo[side, 2 * k + c : 2 * k + c + 1] + (sign * 0.25) * (right - left)
                rhs[k, c, row : row + 1] += factor * term

    @pl.when(has_up)
    def _():
        to_down.wait_recv()
        beside(0, 0, -1.0)

    @pl.when(has_down)
    def _():
        to_up.wait_recv()
        beside(1, rows - 1, 1.0)

    def both(fn):
        loop(layers // 2, layers, fn)
        loop(1, layers // 2, fn)

    loop(layers // 2, layers, send_low)
    loop(1, layers // 2, send_low)
    def send_high(p):
        s = layer ^ p
        pl.semaphore_wait(layer_ready.at[s], 1)
        rhs_copy(s).start()

    loop(layer + 1, layers, send_high)

    both(lambda s: own_copy(s).start())
    here = pl.ds(pl.multiple_of(layer * 128, 128), 128)
    for k in range(per_layer):
        for c in range(2):
            gathered[layer * per_layer + k, c] = rhs[k, c, :, here]

    arrived(cell_rows_in.at[pl.ds(0, layers - 1)], own_recv)
    gate_rows[pl.ds(zc, 1)] = jnp.sum(cell_rows_in[...], axis=0, keepdims=True)
    answers = (NY - 1 - y_rank) * NX + (n_zc - 1 - zc) - (ZHI - 1 - z_hi)

    @pl.when(answers > 0)
    def _():
        pl.semaphore_wait(late_ready, answers)

    def rows_copy(j):
        return remote(gate_rows.at[pl.ds(zc, 1)], gate_rows.at[pl.ds(zc, 1)], rows_send, rows_recv, at_zc(j))

    loop(1, n_zc, lambda j: rows_copy(j).start())

    some = pl.ds(0, (layers - 1) * per_layer)
    most = pl.ds(0, (layers - 1) * 128)
    arrived(gathered.at[some], rhs_recv)
    scaled = [jnp.zeros((rows, 128), F32)] * 2
    for k in range(nz):
        inv = inverse[k]
        for c in range(2):
            r = gathered[k, c]
            scaled[c] = (r + vertical[k - 1] * scaled[c]) * inv if k else r * inv
            solved[k, c] = scaled[c]
    upper = [jnp.zeros((rows, 128), F32)] * 2
    total = jnp.zeros((rows, 128), F32)
    for k in reversed(range(nz)):
        for c in range(2):
            upper[c] = solved[k, c] + ratio[k] * upper[c] if k < nz - 1 else solved[k, c]
            x_new = upper[c] * active
            solved[k, c] = x_new
            total = total + x_new
    table[xy] = total * (1.0 / nz)

    def table_copy(s):
        return remote(table.at[xy], table.at[xy], table_send, table_recv.at[s], at_xy(s))

    loop(n_xy // 2, n_xy, lambda s: table_copy(s).start())
    loop(1, n_xy // 2, lambda s: table_copy(s).start())

    def back_copy(s):
        return remote(
            solved.at[pl.ds((layer ^ s) * per_layer, per_layer)],
            out.at[:, :, :, here],
            back_send,
            back_recv,
            at_layer(s),
        )

    both(lambda s: back_copy(s).start())
    keep = pltpu.make_async_copy(solved.at[pl.ds(layer * per_layer, per_layer)], out.at[:, :, :, here], self_sem)
    keep.start()

    arrived(gate_rows.at[pl.ds(0, n_zc - 1)], rows_recv)
    groups = n_zc // 8
    where, lanes = [], []
    for v in range(groups):
        cell = gate_rows[v * 8 : (v + 1) * 8].astype(jnp.int32)
        row, col = cell // width, cell % width
        t, piece = row // rows, col // 128
        inside = (t % NC == core) & (t // (NC * NY) == z_lo) & (piece // NX == z_hi)
        spot = (((t // NC) % NY) * NX + piece % NX) * rows + row % rows
        where.append(jnp.where(inside, spot, -1))
        lanes.append(col % 128)

    def look(dy, found):
        found = list(found)
        for dx in range(NX):
            s = dy * NX + dx

            @pl.when(s > 0)
            def _():
                table_copy(s).wait_recv()

        for dx in range(NX):
            q = xy ^ (dy * NX + dx)
            for r in range(rows):
                line = jnp.broadcast_to(table[q, r : r + 1], (8, 128))
                for v in range(groups):
                    got = jnp.take_along_axis(line, lanes[v], axis=1, mode="promise_in_bounds")
                    found[v] = jnp.where(where[v] == q * rows + r, got, found[v])
        return tuple(found)

    found = tuple(jnp.zeros((8, 128), F32) for _ in range(groups))
    for low, high in ((0, NY // 2), (NY // 2 + 1, NY), (NY // 2, NY // 2 + 1)):
        found = lax.fori_loop(low, high, look, found)
    for v in range(groups):
        picked[v * 8 : (v + 1) * 8] = found[v]

    def part_copy(j):
        return remote(picked.at[pl.ds(zc_index(j), 1)], parts.at[pl.ds(zc, 1)], part_send, part_recv, at_zc(j))

    loop(1, n_zc, lambda j: part_copy(j).start())
    parts[pl.ds(zc, 1)] = picked[pl.ds(zc, 1)]
    arrived(out.at[:, :, :, most], back_recv)
    keep.wait()

    @pl.when(has_up)
    def _():
        to_up.wait_send()

    @pl.when(has_down)
    def _():
        to_down.wait_send()

    arrived(rhs.at[:, :, :, most], rhs_send)
    arrived(cell_rows_out.at[pl.ds(0, layers - 1)], own_send)
    arrived(gate_rows.at[pl.ds(0, n_zc - 1)], rows_send)
    arrived(table.at[pl.ds(0, n_xy - 1)], table_send)
    arrived(picked.at[pl.ds(0, n_zc - 1)], part_send)
    arrived(solved.at[some], back_send)
    arrived(parts.at[pl.ds(0, n_zc - 1)], part_recv)
    line = jnp.sum(parts[...], axis=0, keepdims=True)
    half = lax.broadcasted_iota(jnp.int32, (1, 128), 1) < 64
    slot0 = jnp.sum(jnp.where(half, line, 0.0), axis=1, keepdims=True)
    slot1 = jnp.sum(jnp.where(half, 0.0, line), axis=1, keepdims=True)
    flux[...] = jnp.where(lax.broadcasted_iota(jnp.int32, (1, 2), 1) == 0, slot0, slot1)


def solution(mesh):
    tiles, layers = mesh.shape["tile"], mesh.shape["layer"]
    n_xy, n_zc = NX * NY, ZHI * ZLO * NC
    assert tiles == ZLO * NY * NC and layers == ZHI * NX

    def local(adjoint, source, viscosity, vertical, friction, ice_mask, gate_cells, gate_owner):
        owner = gate_owner.reshape(-1, 128)
        gate_cells = gate_cells.T
        per_layer, _, rows, width = adjoint.shape
        nz = vertical.shape[0]
        vmem, dma = pltpu.VMEM, pltpu.SemaphoreType.DMA
        scratch = [
            vmem(a.shape, a.dtype)
            for a in (adjoint, source, viscosity, vertical, friction, ice_mask, gate_cells, owner)
        ]
        scratch += [
            vmem((2, 2 * per_layer, width), F32),
            vmem((2, 2 * per_layer, width), F32),
            vmem(adjoint.shape, F32),
            vmem((nz, 2, rows, 128), F32),
            vmem((nz, 2, rows, 128), F32),
            vmem((nz, rows, 128), F32),
            vmem((nz, rows, 128), F32),
            vmem((n_xy, rows, 128), F32),
            vmem((2 * layers, owner.size + 128), F32),
            vmem((gate_cells.shape[0], 128), F32),
            vmem((layers, 128), F32),
            vmem((layers, 128), F32),
            vmem((n_zc, 128), F32),
            vmem((n_zc, 128), F32),
            vmem((n_zc, 128), F32),
            dma((8,)),
        ]
        scratch += [dma((2,)), dma((2,))]
        scratch += [dma] * 6
        scratch += [dma, dma((n_xy,))]
        scratch += [dma] * 4
        plain = pltpu.SemaphoreType.REGULAR
        scratch += [dma, plain, plain((layers,)), plain]
        return pl.pallas_call(
            functools.partial(kernel, tiles, layers),
            out_shape=(
                jax.ShapeDtypeStruct(adjoint.shape, F32),
                jax.ShapeDtypeStruct((1, 2), F32),
            ),
            in_specs=[pl.BlockSpec(memory_space=pltpu.HBM)] * 8,
            out_specs=(
                pl.BlockSpec(memory_space=pl.ANY),
                pl.BlockSpec(memory_space=pltpu.VMEM),
            ),
            scratch_shapes=scratch,
            compiler_params=pltpu.CompilerParams(
                collective_id=0, has_side_effects=True, vmem_limit_bytes=55228 * 1024
            ),
            name="update",
        )(adjoint, source, viscosity, vertical, friction, ice_mask, gate_cells, owner)

    return jax.shard_map(
        local,
        mesh=mesh,
        in_specs=(
            P("layer", None, "tile", None),
            P("layer", None, "tile", None),
            P("layer", "tile", None),
            P(None, "tile", "layer"),
            P("tile", "layer"),
            P("tile", "layer"),
            P("layer", None),
            P(),
        ),
        out_specs=(P("layer", None, "tile", None), P(("tile", "layer"), None)),
        check_vma=False,
    )
```

```python
import functools

import jax
import jax.numpy as jnp
from jax import lax
from jax.experimental import pallas as pl
from jax.experimental.pallas import tpu as pltpu
from jax.sharding import PartitionSpec as P

MESH = pl.DeviceIdType.MESH
SCALE = 0.2
F32 = jnp.float32


NX, NY, ZLO, ZHI, NC = 4, 8, 3, 4, 2


def remote(src, dst, send_sem, recv_sem, device):
    return pltpu.make_async_remote_copy(
        src_ref=src,
        dst_ref=dst,
        send_sem=send_sem,
        recv_sem=recv_sem,
        device_id=device,
        device_id_type=MESH,
    )


def kernel(
    tiles,
    layers,
    adjoint_in,
    source_in,
    viscosity_in,
    vertical_in,
    friction_in,
    mask_in,
    cells_in,
    owner_in,
    out,
    flux,
    adjoint,
    source,
    viscosity,
    vertical,
    friction,
    mask,
    cells,
    owner,
    halo,
    rims,
    rhs,
    gathered,
    solved,
    inverse,
    ratio,
    table,
    select,
    block_cells,
    cell_rows_out,
    cell_rows_in,
    gate_rows,
    picked,
    parts,
    load_sem,
    halo_send,
    halo_recv,
    rhs_send,
    rhs_recv,
    back_send,
    back_recv,
    own_send,
    own_recv,
    table_send,
    table_recv,
    rows_send,
    rows_recv,
    part_send,
    part_recv,
    self_sem,
    halo_ready,
    layer_ready,
    late_ready,
):
    tile = lax.axis_index("tile")
    layer = lax.axis_index("layer")
    nz = vertical.shape[0]
    per_layer = nz // layers
    width = rhs.shape[3]
    rows = rhs.shape[2]
    core, y, z_lo = tile % NC, (tile // NC) % NY, tile // (NC * NY)
    x, z_hi = layer % NX, layer // NX
    xy = y * NX + x
    zc = (z_hi * ZLO + z_lo) * NC + core
    n_xy, n_zc = NX * NY, ZHI * ZLO * NC

    def loop(low, high, fn):
        if isinstance(low, int) and isinstance(high, int):
            for i in range(low, high):
                fn(i)
            return

        def one(i, carry):
            fn(i)
            return carry

        lax.fori_loop(low, high, one, 0)

    def at_layer(s):
        return {"tile": tile, "layer": layer ^ s}

    def at_xy(s):
        return {"tile": tile ^ ((s >> 2) << 1), "layer": layer ^ (s & (NX - 1))}

    def zc_parts(j):
        z = z_lo + (j >> 3)
        return z_hi ^ (j & 3), jnp.where(z >= ZLO, z - ZLO, z), core ^ ((j >> 2) & 1)

    def zc_index(j):
        high, low, c = zc_parts(j)
        return (high * ZLO + low) * NC + c

    def at_zc(j):
        _, low, c = zc_parts(j)
        return {"tile": low * (NY * NC) + (tile & (NY * NC - NC)) + c, "layer": layer ^ ((j & 3) << 2)}

    def rank_of(a):
        return jnp.where(a < NY // 2, a, NY + NY // 2 - 1 - a)

    def signal(sem, device):
        pl.semaphore_signal(sem, inc=1, device_id=device, device_id_type=MESH)

    def arrived(ref, sem):
        pltpu.make_async_copy(ref, ref, sem).wait()

    y_rank = rank_of(y)
    loads = []
    for i, (a, b) in enumerate(
        (
            (adjoint_in, adjoint),
            (source_in, source),
            (viscosity_in, viscosity),
            (vertical_in, vertical),
            (friction_in, friction),
            (mask_in, mask),
            (cells_in, cells),
            (owner_in, owner),
        )
    ):
        copy = pltpu.make_async_copy(a, b, load_sem.at[i])
        copy.start()
        loads.append(copy)

    barrier = pltpu.get_barrier_semaphore()
    has_up, has_down = tile > 0, tile < tiles - 1

    @pl.when(has_down)
    def _():
        signal(barrier, {"tile": tile + 1, "layer": layer})

    def greet_layer(s):
        @pl.when(layer ^ s > layer)
        def _():
            signal(barrier, at_layer(s))

    loop(1, layers, greet_layer)

    def greet_xy(s):
        @pl.when(rank_of(y ^ (s >> 2)) > y_rank)
        def _():
            signal(barrier, at_xy(s))


    def greet_zc(j):
        @pl.when(zc_index(j) > zc)
        def _():
            signal(barrier, at_zc(j))

    loop(ZHI, n_zc, greet_zc)
    loop(NX, n_xy, greet_xy)

    lower = layer + y_rank * NX + zc - z_hi + has_up.astype(jnp.int32)

    @pl.when(lower > 0)
    def _():
        pl.semaphore_wait(barrier, lower)

    @pl.when(has_up)
    def _():
        signal(halo_ready, {"tile": tile - 1, "layer": layer})

    def answer_layer(s):
        @pl.when(layer ^ s < layer)
        def _():
            signal(layer_ready.at[s], at_layer(s))

    loop(layers // 2, layers, answer_layer)
    loop(1, layers // 2, answer_layer)

    to_down = remote(
        rims.at[1],
        halo.at[0],
        halo_send.at[0],
        halo_recv.at[0],
        {"tile": tile + 1, "layer": layer},
    )
    to_up = remote(
        rims.at[0],
        halo.at[1],
        halo_send.at[1],
        halo_recv.at[1],
        {"tile": tile - 1, "layer": layer},
    )
    loads[0].wait()
    for side, row in enumerate((0, rows - 1)):
        for k in range(per_layer):
            for c in range(2):
                rims[side, 2 * k + c : 2 * k + c + 1] = adjoint[k, c, row : row + 1]

    @pl.when(has_up)
    def _():
        to_up.start()

    loads[1].wait()
    loads[2].wait()
    lane = lax.broadcasted_iota(jnp.int32, (1, width), 1)
    first_col, last_col = lane == 0, lane == width - 1
    sub = lax.broadcasted_iota(jnp.int32, (rows, 1), 0)

    def sideways(a):
        left = jnp.where(first_col, 0.0, pltpu.roll(a, 1, 1))
        right = jnp.where(last_col, 0.0, pltpu.roll(a, width - 1, 1))
        return left, right

    for k in range(per_layer):
        coef = SCALE * viscosity[k]
        value, diff, flat = [], [], []
        for c in range(2):
            a = adjoint[k, c]
            left, right = sideways(a)
            value.append(a)
            diff.append(0.25 * (right - left))
            flat.append(left + right - 4.0 * a)
        for c in range(2):
            above = jnp.where(sub == 0, 0.0, pltpu.roll(value[c] - diff[1 - c], 1, 0))
            below = jnp.where(sub == rows - 1, 0.0, pltpu.roll(value[c] + diff[1 - c], rows - 1, 0))
            rhs[k, c] = source[k, c] + coef * (flat[c] + (above + below))

    def rhs_copy(s):
        peer = layer ^ s
        return remote(
            rhs.at[:, :, :, pl.ds(pl.multiple_of(peer * 128, 128), 128)],
            gathered.at[pl.ds(layer * per_layer, per_layer)],
            rhs_send,
            rhs_recv,
            at_layer(s),
        )

    def own_copy(s):
        return remote(
            cell_rows_out.at[pl.ds(layer ^ s, 1)],
            cell_rows_in.at[pl.ds(layer, 1)],
            own_send,
            own_recv,
            at_layer(s),
        )

    def send_low(s):
        @pl.when(layer ^ s < layer)
        def _():
            rhs_copy(s).start()
            own_copy(s).start()


    def answer_xy(s):
        @pl.when(rank_of(y ^ (s >> 2)) < y_rank)
        def _():
            signal(late_ready, at_xy(s))

    def answer_zc(j):
        @pl.when(zc_index(j) < zc)
        def _():
            signal(late_ready, at_zc(j))

    loop(NX, n_xy, answer_xy)
    loop(ZHI, n_zc, answer_zc)

    for c in loads[3:]:
        c.wait()
    count = cells.shape[1]
    gates = owner.shape[0] * 128
    owner_ids = tile * layers + lax.broadcasted_iota(jnp.int32, (layers, 128), 0)
    lane128 = lax.broadcasted_iota(jnp.int32, (layers, 128), 1)
    far = jnp.full((layers, 128), gates, jnp.int32)
    for j in range(owner.shape[0]):
        mine = owner[pl.ds(j, 1), :] == owner_ids
        far = jnp.minimum(far, jnp.where(mine, lane128 + j * 128, gates))
    first = jnp.min(far, axis=1, keepdims=True)
    for j in range(owner.shape[0]):
        mine = owner[pl.ds(j, 1), :] == owner_ids
        is_first = (lane128 + j * 128) == first
        select[0:layers, j * 128 : (j + 1) * 128] = jnp.where(mine & is_first, 1.0, 0.0)
        select[layers : 2 * layers, j * 128 : (j + 1) * 128] = jnp.where(
            mine & jnp.logical_not(is_first), 1.0, 0.0
        )
    select[:, gates:] = jnp.zeros((2 * layers, select.shape[1] - gates), F32)
    base = (layer * count) // 128
    shift = layer * count - base * 128
    block_cells[...] = jnp.zeros_like(block_cells)
    block_cells[:, 0:count] = cells[...].astype(F32)
    window = select[:, pl.ds(pl.multiple_of(base * 128, 128), 256)]
    window = pltpu.roll(window, lax.rem(256 - shift, 256), 1)[:, 0:128]
    chosen = lax.dot_general(
        window,
        block_cells[...],
        (((1,), (1,)), ((), ())),
        precision=lax.Precision.HIGHEST,
        preferred_element_type=F32,
    )
    cell_rows_out[...] = jnp.concatenate([chosen[0:layers], chosen[layers:]], axis=1)
    cell_rows_in[pl.ds(layer, 1)] = cell_rows_out[pl.ds(layer, 1)]

    active = mask[...].astype(F32)
    beneath = friction[...]
    link = jnp.zeros_like(beneath)
    ratio_prev = jnp.zeros_like(beneath)
    for k in range(nz):
        v = vertical[k]
        inv = 1.0 / (1.0 + beneath + v - link * ratio_prev)
        ratio_prev = v * inv
        inverse[k] = inv
        ratio[k] = ratio_prev
        beneath = v
        link = v

    @pl.when(has_down)
    def _():
        pl.semaphore_wait(halo_ready, 1)
        to_down.start()

    def beside(side, row, sign):
        for k in range(per_layer):
            factor = SCALE * viscosity[k, row : row + 1]
            for c in range(2):
                left, right = sideways(halo[side, 2 * k + 1 - c : 2 * k + 2 - c])
                term = halo[side, 2 * k + c : 2 * k + c + 1] + (sign * 0.25) * (right - left)
                rhs[k, c, row : row + 1] += factor * term

    @pl.when(has_up)
    def _():
        to_down.wait_recv()
        beside(0, 0, -1.0)

    @pl.when(has_down)
    def _():
        to_up.wait_recv()
        beside(1, rows - 1, 1.0)

    def both(fn):
        loop(layers // 2, layers, fn)
        loop(1, layers // 2, fn)

    loop(layers // 2, layers, send_low)
    loop(1, layers // 2, send_low)
    def send_high(p):
        s = layer ^ p
        pl.semaphore_wait(layer_ready.at[s], 1)
        rhs_copy(s).start()
        own_copy(s).start()

    loop(layer + 1, layers, send_high)

    here = pl.ds(pl.multiple_of(layer * 128, 128), 128)
    for k in range(per_layer):
        for c in range(2):
            gathered[layer * per_layer + k, c] = rhs[k, c, :, here]

    arrived(cell_rows_in.at[pl.ds(0, layers - 1)], own_recv)
    gate_rows[pl.ds(zc, 1)] = jnp.sum(cell_rows_in[...], axis=0, keepdims=True)
    answers = (NY - 1 - y_rank) * NX + (n_zc - 1 - zc) - (ZHI - 1 - z_hi)

    @pl.when(answers > 0)
    def _():
        pl.semaphore_wait(late_ready, answers)

    def rows_copy(j):
        return remote(gate_rows.at[pl.ds(zc, 1)], gate_rows.at[pl.ds(zc, 1)], rows_send, rows_recv, at_zc(j))

    loop(1, n_zc, lambda j: rows_copy(j).start())

    some = pl.ds(0, (layers - 1) * per_layer)
    most = pl.ds(0, (layers - 1) * 128)
    arrived(gathered.at[some], rhs_recv)
    scaled = [jnp.zeros((rows, 128), F32)] * 2
    for k in range(nz):
        inv = inverse[k]
        for c in range(2):
            r = gathered[k, c]
            scaled[c] = (r + vertical[k - 1] * scaled[c]) * inv if k else r * inv
            solved[k, c] = scaled[c]
    upper = [jnp.zeros((rows, 128), F32)] * 2
    total = jnp.zeros((rows, 128), F32)
    for k in reversed(range(nz)):
        for c in range(2):
            upper[c] = solved[k, c] + ratio[k] * upper[c] if k < nz - 1 else solved[k, c]
            x_new = upper[c] * active
            solved[k, c] = x_new
            total = total + x_new
    table[xy] = total * (1.0 / nz)

    def table_copy(s):
        return remote(table.at[xy], table.at[xy], table_send, table_recv.at[s], at_xy(s))

    loop(n_xy // 2, n_xy, lambda s: table_copy(s).start())
    loop(1, n_xy // 2, lambda s: table_copy(s).start())

    def back_copy(s):
        return remote(
            solved.at[pl.ds((layer ^ s) * per_layer, per_layer)],
            out.at[:, :, :, here],
            back_send,
            back_recv,
            at_layer(s),
        )

    both(lambda s: back_copy(s).start())
    keep = pltpu.make_async_copy(solved.at[pl.ds(layer * per_layer, per_layer)], out.at[:, :, :, here], self_sem)
    keep.start()

    arrived(gate_rows.at[pl.ds(0, n_zc - 1)], rows_recv)
    groups = n_zc // 8
    where, lanes = [], []
    for v in range(groups):
        cell = gate_rows[v * 8 : (v + 1) * 8].astype(jnp.int32)
        row, col = cell // width, cell % width
        t, piece = row // rows, col // 128
        inside = (t % NC == core) & (t // (NC * NY) == z_lo) & (piece // NX == z_hi)
        spot = (((t // NC) % NY) * NX + piece % NX) * rows + row % rows
        where.append(jnp.where(inside, spot, -1))
        lanes.append(col % 128)

    def look(dy, found):
        found = list(found)
        for dx in range(NX):
            s = dy * NX + dx

            @pl.when(s > 0)
            def _():
                table_copy(s).wait_recv()

        for dx in range(NX):
            q = xy ^ (dy * NX + dx)
            for r in range(rows):
                line = jnp.broadcast_to(table[q, r : r + 1], (8, 128))
                for v in range(groups):
                    got = jnp.take_along_axis(line, lanes[v], axis=1, mode="promise_in_bounds")
                    found[v] = jnp.where(where[v] == q * rows + r, got, found[v])
        return tuple(found)

    found = tuple(jnp.zeros((8, 128), F32) for _ in range(groups))
    for low, high in ((0, NY // 2), (NY // 2 + 1, NY), (NY // 2, NY // 2 + 1)):
        found = lax.fori_loop(low, high, look, found)
    for v in range(groups):
        picked[v * 8 : (v + 1) * 8] = found[v]

    def part_copy(j):
        return remote(picked.at[pl.ds(zc_index(j), 1)], parts.at[pl.ds(zc, 1)], part_send, part_recv, at_zc(j))

    loop(1, n_zc, lambda j: part_copy(j).start())
    parts[pl.ds(zc, 1)] = picked[pl.ds(zc, 1)]
    arrived(out.at[:, :, :, most], back_recv)
    keep.wait()

    @pl.when(has_up)
    def _():
        to_up.wait_send()

    @pl.when(has_down)
    def _():
        to_down.wait_send()

    arrived(rhs.at[:, :, :, most], rhs_send)
    arrived(cell_rows_out.at[pl.ds(0, layers - 1)], own_send)
    arrived(gate_rows.at[pl.ds(0, n_zc - 1)], rows_send)
    arrived(table.at[pl.ds(0, n_xy - 1)], table_send)
    arrived(picked.at[pl.ds(0, n_zc - 1)], part_send)
    arrived(solved.at[some], back_send)
    arrived(parts.at[pl.ds(0, n_zc - 1)], part_recv)
    line = jnp.sum(parts[...], axis=0, keepdims=True)
    half = lax.broadcasted_iota(jnp.int32, (1, 128), 1) < 64
    slot0 = jnp.sum(jnp.where(half, line, 0.0), axis=1, keepdims=True)
    slot1 = jnp.sum(jnp.where(half, 0.0, line), axis=1, keepdims=True)
    flux[...] = jnp.where(lax.broadcasted_iota(jnp.int32, (1, 2), 1) == 0, slot0, slot1)


def solution(mesh):
    tiles, layers = mesh.shape["tile"], mesh.shape["layer"]
    n_xy, n_zc = NX * NY, ZHI * ZLO * NC
    assert tiles == ZLO * NY * NC and layers == ZHI * NX

    def local(adjoint, source, viscosity, vertical, friction, ice_mask, gate_cells, gate_owner):
        owner = gate_owner.reshape(-1, 128)
        gate_cells = gate_cells.T
        per_layer, _, rows, width = adjoint.shape
        nz = vertical.shape[0]
        vmem, dma = pltpu.VMEM, pltpu.SemaphoreType.DMA
        scratch = [
            vmem(a.shape, a.dtype)
            for a in (adjoint, source, viscosity, vertical, friction, ice_mask, gate_cells, owner)
        ]
        scratch += [
            vmem((2, 2 * per_layer, width), F32),
            vmem((2, 2 * per_layer, width), F32),
            vmem(adjoint.shape, F32),
            vmem((nz, 2, rows, 128), F32),
            vmem((nz, 2, rows, 128), F32),
            vmem((nz, rows, 128), F32),
            vmem((nz, rows, 128), F32),
            vmem((n_xy, rows, 128), F32),
            vmem((2 * layers, owner.size + 128), F32),
            vmem((gate_cells.shape[0], 128), F32),
            vmem((layers, 128), F32),
            vmem((layers, 128), F32),
            vmem((n_zc, 128), F32),
            vmem((n_zc, 128), F32),
            vmem((n_zc, 128), F32),
            dma((8,)),
        ]
        scratch += [dma((2,)), dma((2,))]
        scratch += [dma] * 6
        scratch += [dma, dma((n_xy,))]
        scratch += [dma] * 4
        plain = pltpu.SemaphoreType.REGULAR
        scratch += [dma, plain, plain((layers,)), plain]
        return pl.pallas_call(
            functools.partial(kernel, tiles, layers),
            out_shape=(
                jax.ShapeDtypeStruct(adjoint.shape, F32),
                jax.ShapeDtypeStruct((1, 2), F32),
            ),
            in_specs=[pl.BlockSpec(memory_space=pltpu.HBM)] * 8,
            out_specs=(
                pl.BlockSpec(memory_space=pl.ANY),
                pl.BlockSpec(memory_space=pltpu.VMEM),
            ),
            scratch_shapes=scratch,
            compiler_params=pltpu.CompilerParams(
                collective_id=0, has_side_effects=True, vmem_limit_bytes=55228 * 1024
            ),
            name="update",
        )(adjoint, source, viscosity, vertical, friction, ice_mask, gate_cells, owner)

    return jax.shard_map(
        local,
        mesh=mesh,
        in_specs=(
            P("layer", None, "tile", None),
            P("layer", None, "tile", None),
            P("layer", "tile", None),
            P(None, "tile", "layer"),
            P("tile", "layer"),
            P("tile", "layer"),
            P("layer", None),
            P(),
        ),
        out_specs=(P("layer", None, "tile", None), P(("tile", "layer"), None)),
        check_vma=False,
    )
```

```python
import functools

import jax
import jax.numpy as jnp
from jax import lax
from jax.experimental import pallas as pl
from jax.experimental.pallas import tpu as pltpu
from jax.sharding import PartitionSpec as P

MESH = pl.DeviceIdType.MESH
SCALE = 0.2
F32 = jnp.float32


NX, NY, ZLO, ZHI, NC = 4, 8, 3, 4, 2


def remote(src, dst, send_sem, recv_sem, device):
    return pltpu.make_async_remote_copy(
        src_ref=src,
        dst_ref=dst,
        send_sem=send_sem,
        recv_sem=recv_sem,
        device_id=device,
        device_id_type=MESH,
    )


def kernel(
    tiles,
    layers,
    adjoint_in,
    source_in,
    viscosity_in,
    vertical_in,
    friction_in,
    mask_in,
    cells_in,
    owner_in,
    out,
    flux,
    adjoint,
    source,
    viscosity,
    vertical,
    friction,
    mask,
    cells,
    owner,
    halo,
    rims,
    rhs,
    gathered,
    solved,
    inverse,
    ratio,
    table,
    select,
    block_cells,
    cell_rows_out,
    cell_rows_in,
    gate_rows,
    picked,
    parts,
    load_sem,
    halo_send,
    halo_recv,
    rhs_send,
    rhs_recv,
    back_send,
    back_recv,
    own_send,
    own_recv,
    table_send,
    table_recv,
    rows_send,
    rows_recv,
    part_send,
    part_recv,
    self_sem,
    halo_ready,
    layer_ready,
    late_ready,
):
    tile = lax.axis_index("tile")
    layer = lax.axis_index("layer")
    nz = vertical.shape[0]
    per_layer = nz // layers
    width = rhs.shape[3]
    rows = rhs.shape[2]
    core, y, z_lo = tile % NC, (tile // NC) % NY, tile // (NC * NY)
    x, z_hi = layer % NX, layer // NX
    xy = y * NX + x
    zc = (z_hi * ZLO + z_lo) * NC + core
    n_xy, n_zc = NX * NY, ZHI * ZLO * NC

    def loop(low, high, fn):
        if isinstance(low, int) and isinstance(high, int):
            for i in range(low, high):
                fn(i)
            return

        def one(i, carry):
            fn(i)
            return carry

        lax.fori_loop(low, high, one, 0)

    def at_layer(s):
        return {"tile": tile, "layer": layer ^ s}

    def at_xy(s):
        return {"tile": tile ^ ((s >> 2) << 1), "layer": layer ^ (s & (NX - 1))}

    def zc_parts(j):
        z = z_lo + (j >> 3)
        return z_hi ^ (j & 3), jnp.where(z >= ZLO, z - ZLO, z), core ^ ((j >> 2) & 1)

    def zc_index(j):
        high, low, c = zc_parts(j)
        return (high * ZLO + low) * NC + c

    def at_zc(j):
        _, low, c = zc_parts(j)
        return {"tile": low * (NY * NC) + (tile & (NY * NC - NC)) + c, "layer": layer ^ ((j & 3) << 2)}

    def rank_of(a):
        return jnp.where(a < NY // 2, a, NY + NY // 2 - 1 - a)

    def signal(sem, device):
        pl.semaphore_signal(sem, inc=1, device_id=device, device_id_type=MESH)

    def arrived(ref, sem):
        pltpu.make_async_copy(ref, ref, sem).wait()

    y_rank = rank_of(y)
    loads = []
    for i, (a, b) in enumerate(
        (
            (adjoint_in, adjoint),
            (source_in, source),
            (viscosity_in, viscosity),
            (vertical_in, vertical),
            (friction_in, friction),
            (mask_in, mask),
            (cells_in, cells),
            (owner_in, owner),
        )
    ):
        copy = pltpu.make_async_copy(a, b, load_sem.at[i])
        copy.start()
        loads.append(copy)

    barrier = pltpu.get_barrier_semaphore()
    has_up, has_down = tile > 0, tile < tiles - 1

    @pl.when(has_down)
    def _():
        signal(barrier, {"tile": tile + 1, "layer": layer})

    def greet_layer(s):
        @pl.when(layer ^ s > layer)
        def _():
            signal(barrier, at_layer(s))

    loop(1, layers, greet_layer)

    def greet_xy(s):
        @pl.when(rank_of(y ^ (s >> 2)) > y_rank)
        def _():
            signal(barrier, at_xy(s))


    def greet_zc(j):
        @pl.when(zc_index(j) > zc)
        def _():
            signal(barrier, at_zc(j))

    loop(ZHI, n_zc, greet_zc)
    loop(NX, n_xy, greet_xy)

    lower = layer + y_rank * NX + zc - z_hi + has_up.astype(jnp.int32)

    @pl.when(lower > 0)
    def _():
        pl.semaphore_wait(barrier, lower)

    @pl.when(has_up)
    def _():
        signal(halo_ready, {"tile": tile - 1, "layer": layer})

    def answer_layer(s):
        @pl.when(layer ^ s < layer)
        def _():
            signal(layer_ready.at[s], at_layer(s))

    loop(layers // 2, layers, answer_layer)
    loop(1, layers // 2, answer_layer)

    to_down = remote(
        rims.at[1],
        halo.at[0],
        halo_send.at[0],
        halo_recv.at[0],
        {"tile": tile + 1, "layer": layer},
    )
    to_up = remote(
        rims.at[0],
        halo.at[1],
        halo_send.at[1],
        halo_recv.at[1],
        {"tile": tile - 1, "layer": layer},
    )
    loads[0].wait()
    for side, row in enumerate((0, rows - 1)):
        for k in range(per_layer):
            for c in range(2):
                rims[side, 2 * k + c : 2 * k + c + 1] = adjoint[k, c, row : row + 1]

    @pl.when(has_up)
    def _():
        to_up.start()

    loads[1].wait()
    loads[2].wait()
    lane = lax.broadcasted_iota(jnp.int32, (1, width), 1)
    first_col, last_col = lane == 0, lane == width - 1
    sub = lax.broadcasted_iota(jnp.int32, (rows, 1), 0)

    def sideways(a):
        left = jnp.where(first_col, 0.0, pltpu.roll(a, 1, 1))
        right = jnp.where(last_col, 0.0, pltpu.roll(a, width - 1, 1))
        return left, right

    for k in range(per_layer):
        coef = SCALE * viscosity[k]
        value, diff, flat = [], [], []
        for c in range(2):
            a = adjoint[k, c]
            left, right = sideways(a)
            value.append(a)
            diff.append(0.25 * (right - left))
            flat.append(left + right - 4.0 * a)
        for c in range(2):
            above = jnp.where(sub == 0, 0.0, pltpu.roll(value[c] - diff[1 - c], 1, 0))
            below = jnp.where(sub == rows - 1, 0.0, pltpu.roll(value[c] + diff[1 - c], rows - 1, 0))
            rhs[k, c] = source[k, c] + coef * (flat[c] + (above + below))

    def rhs_copy(s):
        peer = layer ^ s
        return remote(
            rhs.at[:, :, :, pl.ds(pl.multiple_of(peer * 128, 128), 128)],
            gathered.at[pl.ds(layer * per_layer, per_layer)],
            rhs_send,
            rhs_recv,
            at_layer(s),
        )

    def own_copy(s):
        return remote(
            cell_rows_out.at[pl.ds(layer ^ s, 1)],
            cell_rows_in.at[pl.ds(layer, 1)],
            own_send,
            own_recv,
            at_layer(s),
        )

    def send_low(s):
        @pl.when(layer ^ s < layer)
        def _():
            rhs_copy(s).start()
            own_copy(s).start()


    def answer_xy(s):
        @pl.when(rank_of(y ^ (s >> 2)) < y_rank)
        def _():
            signal(late_ready, at_xy(s))

    def answer_zc(j):
        @pl.when(zc_index(j) < zc)
        def _():
            signal(late_ready, at_zc(j))

    loop(NX, n_xy, answer_xy)
    loop(ZHI, n_zc, answer_zc)

    for c in loads[3:]:
        c.wait()
    count = cells.shape[1]
    gates = owner.shape[0] * 128
    owner_ids = tile * layers + lax.broadcasted_iota(jnp.int32, (layers, 128), 0)
    lane128 = lax.broadcasted_iota(jnp.int32, (layers, 128), 1)
    far = jnp.full((layers, 128), gates, jnp.int32)
    for j in range(owner.shape[0]):
        mine = owner[pl.ds(j, 1), :] == owner_ids
        far = jnp.minimum(far, jnp.where(mine, lane128 + j * 128, gates))
    first = jnp.min(far, axis=1, keepdims=True)
    for j in range(owner.shape[0]):
        mine = owner[pl.ds(j, 1), :] == owner_ids
        is_first = (lane128 + j * 128) == first
        select[0:layers, j * 128 : (j + 1) * 128] = jnp.where(mine & is_first, 1.0, 0.0)
        select[layers : 2 * layers, j * 128 : (j + 1) * 128] = jnp.where(
            mine & jnp.logical_not(is_first), 1.0, 0.0
        )
    select[:, gates:] = jnp.zeros((2 * layers, select.shape[1] - gates), F32)
    base = (layer * count) // 128
    shift = layer * count - base * 128
    block_cells[...] = jnp.zeros_like(block_cells)
    block_cells[:, 0:count] = cells[...].astype(F32)
    window = select[:, pl.ds(pl.multiple_of(base * 128, 128), 256)]
    window = pltpu.roll(window, lax.rem(256 - shift, 256), 1)[:, 0:128]
    chosen = lax.dot_general(
        window,
        block_cells[...],
        (((1,), (1,)), ((), ())),
        precision=lax.Precision.HIGHEST,
        preferred_element_type=F32,
    )
    cell_rows_out[...] = jnp.concatenate([chosen[0:layers], chosen[layers:]], axis=1)
    cell_rows_in[pl.ds(layer, 1)] = cell_rows_out[pl.ds(layer, 1)]

    active = mask[...].astype(F32)
    beneath = friction[...]
    link = jnp.zeros_like(beneath)
    ratio_prev = jnp.zeros_like(beneath)
    for k in range(nz):
        v = vertical[k]
        inv = 1.0 / (1.0 + beneath + v - link * ratio_prev)
        ratio_prev = v * inv
        inverse[k] = inv
        ratio[k] = ratio_prev
        beneath = v
        link = v

    @pl.when(has_down)
    def _():
        pl.semaphore_wait(halo_ready, 1)
        to_down.start()

    def beside(side, row, sign):
        for k in range(per_layer):
            factor = SCALE * viscosity[k, row : row + 1]
            for c in range(2):
                left, right = sideways(halo[side, 2 * k + 1 - c : 2 * k + 2 - c])
                term = halo[side, 2 * k + c : 2 * k + c + 1] + (sign * 0.25) * (right - left)
                rhs[k, c, row : row + 1] += factor * term

    @pl.when(has_up)
    def _():
        to_down.wait_recv()
        beside(0, 0, -1.0)

    @pl.when(has_down)
    def _():
        to_up.wait_recv()
        beside(1, rows - 1, 1.0)

    def both(fn):
        loop(layers // 2, layers, fn)
        loop(1, layers // 2, fn)

    loop(layers // 2, layers, send_low)
    loop(1, layers // 2, send_low)
    def send_high(p):
        s = layer ^ p
        pl.semaphore_wait(layer_ready.at[s], 1)
        rhs_copy(s).start()
        own_copy(s).start()

    loop(layer + 1, layers, send_high)

    here = pl.ds(pl.multiple_of(layer * 128, 128), 128)
    for k in range(per_layer):
        for c in range(2):
            gathered[layer * per_layer + k, c] = rhs[k, c, :, here]

    arrived(cell_rows_in.at[pl.ds(0, layers - 1)], own_recv)
    gate_rows[pl.ds(zc, 1)] = jnp.sum(cell_rows_in[...], axis=0, keepdims=True)
    answers = (NY - 1 - y_rank) * NX + (n_zc - 1 - zc) - (ZHI - 1 - z_hi)

    @pl.when(answers > 0)
    def _():
        pl.semaphore_wait(late_ready, answers)

    def rows_copy(j):
        return remote(gate_rows.at[pl.ds(zc, 1)], gate_rows.at[pl.ds(zc, 1)], rows_send, rows_recv, at_zc(j))

    loop(1, n_zc, lambda j: rows_copy(j).start())

    some = pl.ds(0, (layers - 1) * per_layer)
    most = pl.ds(0, (layers - 1) * 128)
    arrived(gathered.at[some], rhs_recv)
    scaled = [jnp.zeros((rows, 128), F32)] * 2
    for k in range(nz):
        inv = inverse[k]
        for c in range(2):
            r = gathered[k, c]
            scaled[c] = (r + vertical[k - 1] * scaled[c]) * inv if k else r * inv
            solved[k, c] = scaled[c]
    upper = [jnp.zeros((rows, 128), F32)] * 2
    total = jnp.zeros((rows, 128), F32)
    for k in reversed(range(nz)):
        for c in range(2):
            upper[c] = solved[k, c] + ratio[k] * upper[c] if k < nz - 1 else solved[k, c]
            x_new = upper[c] * active
            solved[k, c] = x_new
            total = total + x_new
    table[xy] = total * (1.0 / nz)

    def table_copy(s):
        return remote(table.at[xy], table.at[xy], table_send, table_recv.at[s], at_xy(s))

    loop(n_xy // 2, n_xy, lambda s: table_copy(s).start())

    def back_copy(s):
        return remote(
            solved.at[pl.ds((layer ^ s) * per_layer, per_layer)],
            out.at[:, :, :, here],
            back_send,
            back_recv,
            at_layer(s),
        )

    both(lambda s: back_copy(s).start())
    loop(1, n_xy // 2, lambda s: table_copy(s).start())
    keep = pltpu.make_async_copy(solved.at[pl.ds(layer * per_layer, per_layer)], out.at[:, :, :, here], self_sem)
    keep.start()

    arrived(gate_rows.at[pl.ds(0, n_zc - 1)], rows_recv)
    groups = n_zc // 8
    where, lanes = [], []
    for v in range(groups):
        cell = gate_rows[v * 8 : (v + 1) * 8].astype(jnp.int32)
        row, col = cell // width, cell % width
        t, piece = row // rows, col // 128
        inside = (t % NC == core) & (t // (NC * NY) == z_lo) & (piece // NX == z_hi)
        spot = (((t // NC) % NY) * NX + piece % NX) * rows + row % rows
        where.append(jnp.where(inside, spot, -1))
        lanes.append(col % 128)

    def look(dy, found):
        found = list(found)
        for dx in range(NX):
            s = dy * NX + dx

            @pl.when(s > 0)
            def _():
                table_copy(s).wait_recv()

        for dx in range(NX):
            q = xy ^ (dy * NX + dx)
            for r in range(rows):
                line = jnp.broadcast_to(table[q, r : r + 1], (8, 128))
                for v in range(groups):
                    got = jnp.take_along_axis(line, lanes[v], axis=1, mode="promise_in_bounds")
                    found[v] = jnp.where(where[v] == q * rows + r, got, found[v])
        return tuple(found)

    found = tuple(jnp.zeros((8, 128), F32) for _ in range(groups))
    for low, high in ((0, NY // 2), (NY // 2 + 1, NY), (NY // 2, NY // 2 + 1)):
        found = lax.fori_loop(low, high, look, found)
    for v in range(groups):
        picked[v * 8 : (v + 1) * 8] = found[v]

    def part_copy(j):
        return remote(picked.at[pl.ds(zc_index(j), 1)], parts.at[pl.ds(zc, 1)], part_send, part_recv, at_zc(j))

    loop(1, n_zc, lambda j: part_copy(j).start())
    parts[pl.ds(zc, 1)] = picked[pl.ds(zc, 1)]
    arrived(out.at[:, :, :, most], back_recv)
    keep.wait()

    @pl.when(has_up)
    def _():
        to_up.wait_send()

    @pl.when(has_down)
    def _():
        to_down.wait_send()

    arrived(rhs.at[:, :, :, most], rhs_send)
    arrived(cell_rows_out.at[pl.ds(0, layers - 1)], own_send)
    arrived(gate_rows.at[pl.ds(0, n_zc - 1)], rows_send)
    arrived(table.at[pl.ds(0, n_xy - 1)], table_send)
    arrived(picked.at[pl.ds(0, n_zc - 1)], part_send)
    arrived(solved.at[some], back_send)
    arrived(parts.at[pl.ds(0, n_zc - 1)], part_recv)
    line = jnp.sum(parts[...], axis=0, keepdims=True)
    half = lax.broadcasted_iota(jnp.int32, (1, 128), 1) < 64
    slot0 = jnp.sum(jnp.where(half, line, 0.0), axis=1, keepdims=True)
    slot1 = jnp.sum(jnp.where(half, 0.0, line), axis=1, keepdims=True)
    flux[...] = jnp.where(lax.broadcasted_iota(jnp.int32, (1, 2), 1) == 0, slot0, slot1)


def solution(mesh):
    tiles, layers = mesh.shape["tile"], mesh.shape["layer"]
    n_xy, n_zc = NX * NY, ZHI * ZLO * NC
    assert tiles == ZLO * NY * NC and layers == ZHI * NX

    def local(adjoint, source, viscosity, vertical, friction, ice_mask, gate_cells, gate_owner):
        owner = gate_owner.reshape(-1, 128)
        gate_cells = gate_cells.T
        per_layer, _, rows, width = adjoint.shape
        nz = vertical.shape[0]
        vmem, dma = pltpu.VMEM, pltpu.SemaphoreType.DMA
        scratch = [
            vmem(a.shape, a.dtype)
            for a in (adjoint, source, viscosity, vertical, friction, ice_mask, gate_cells, owner)
        ]
        scratch += [
            vmem((2, 2 * per_layer, width), F32),
            vmem((2, 2 * per_layer, width), F32),
            vmem(adjoint.shape, F32),
            vmem((nz, 2, rows, 128), F32),
            vmem((nz, 2, rows, 128), F32),
            vmem((nz, rows, 128), F32),
            vmem((nz, rows, 128), F32),
            vmem((n_xy, rows, 128), F32),
            vmem((2 * layers, owner.size + 128), F32),
            vmem((gate_cells.shape[0], 128), F32),
            vmem((layers, 128), F32),
            vmem((layers, 128), F32),
            vmem((n_zc, 128), F32),
            vmem((n_zc, 128), F32),
            vmem((n_zc, 128), F32),
            dma((8,)),
        ]
        scratch += [dma((2,)), dma((2,))]
        scratch += [dma] * 6
        scratch += [dma, dma((n_xy,))]
        scratch += [dma] * 4
        plain = pltpu.SemaphoreType.REGULAR
        scratch += [dma, plain, plain((layers,)), plain]
        return pl.pallas_call(
            functools.partial(kernel, tiles, layers),
            out_shape=(
                jax.ShapeDtypeStruct(adjoint.shape, F32),
                jax.ShapeDtypeStruct((1, 2), F32),
            ),
            in_specs=[pl.BlockSpec(memory_space=pltpu.HBM)] * 8,
            out_specs=(
                pl.BlockSpec(memory_space=pl.ANY),
                pl.BlockSpec(memory_space=pltpu.VMEM),
            ),
            scratch_shapes=scratch,
            compiler_params=pltpu.CompilerParams(
                collective_id=0, has_side_effects=True, vmem_limit_bytes=55228 * 1024
            ),
            name="update",
        )(adjoint, source, viscosity, vertical, friction, ice_mask, gate_cells, owner)

    return jax.shard_map(
        local,
        mesh=mesh,
        in_specs=(
            P("layer", None, "tile", None),
            P("layer", None, "tile", None),
            P("layer", "tile", None),
            P(None, "tile", "layer"),
            P("tile", "layer"),
            P("tile", "layer"),
            P("layer", None),
            P(),
        ),
        out_specs=(P("layer", None, "tile", None), P(("tile", "layer"), None)),
        check_vma=False,
    )
```
